32 devices in a mesh: space: 8 (over z, y), dp: 4 (over x, core).
Axes of the slice: x: 2, y: 2, z: 4, core: 2. Of those that a mesh axis runs over, the one named last changes fastest.
Arguments:
- features: bfloat16 [4, 8, 512, 128], P('dp', 'space'), may hold values from -6 to 6
- occupancy: int32 [4, 8, 512], P('dp', 'space'), may hold values from 0 to 1, as said below
- labels: int32 [4, 8, 512], P('dp', 'space'), may hold values from 0 to 2
- rulebook: int32 [4, 8, 27], P('dp', 'space'), may hold values from 0 to 3, as said below
- filter_one: bfloat16 [27, 128, 128], replicated, may hold values from -0.109375 to 0.109375
- filter_two: bfloat16 [27, 128, 128], replicated, may hold values from -0.109375 to 0.109375
- head_weight: bfloat16 [128, 3], replicated, may hold values from -1.5 to 1.5
Outputs:
- grad_filter_one: float32 [27, 128, 128], replicated
- grad_filter_two: float32 [27, 128, 128], replicated
- grad_head: float32 [128, 3], replicated
- mean_loss: float32 [], replicated
- grad_features: bfloat16 [4, 8, 512, 128], P('dp', 'space')
The draws below stay inside these ranges and needn't reach their ends.
Inputs may be any that keep to these rules, and one draw needn't show every extreme that they name: `rulebook`: values below 1 name a slot of the same device, 1 to 1 a slot of the device one lower along space and only for offsets with z displacement -1, 2 to 2 a slot of the device one higher and only for z displacement +1, 3 no neighbour; the first device has no lower and the last no higher references; offset 13 names the slot itself. Each device fills its slots from slot 0 on; unfilled slots have no neighbours and no occupied voxels. `occupancy`: occupied voxels lie only in filled slots; slot 0 of every device is filled and its first voxel occupied; in each crop some device fills all 1 slots.
All inputs are finite; a program needn't handle non-finite values.
Results may differ from the reference program's by a relative error of at most 0.007.
Values may be sent and summed in bfloat16 or wider, within the bound.
No kernel may reach another device: no remote copies, remote signals or barrier semaphores. Data moves between devices by JAX's collectives and lax.ppermute only.
A program may use at most 64 MiB of HBM per device.

```python
from functools import partial
import jax
import jax.numpy as jnp
from jax import lax

C = 128
CLASSES = 3
EDGE = 8
BLK_DEV = 1
VOX = 512
SLOTS = 8
N_SPACE = 8
N_DP = 4


def live_counts(key):
    base_key = jax.random.fold_in(key, 11)
    counts = jax.random.randint(base_key, (N_DP, N_SPACE), 1, BLK_DEV + 1)
    fullest = jax.random.randint(jax.random.fold_in(base_key, 1), (N_DP, 1), 0, N_SPACE)
    places = jnp.arange(N_SPACE, dtype=jnp.int32)[None, :]
    return jnp.where(places == fullest, BLK_DEV, counts).astype(jnp.int32)


def draw_occupancy(key, part):
    counts = live_counts(key)
    slot_ids = jnp.arange(BLK_DEV, dtype=jnp.int32)
    live_slot = slot_ids[None, None, :] < counts[:, :, None]
    voxel_draw = jax.random.randint(jax.random.fold_in(key, 21), (N_DP, N_SPACE, BLK_DEV, VOX), 0, 5)
    filled = (voxel_draw < 3).astype(jnp.int32)
    anchor = (jnp.arange(VOX, dtype=jnp.int32)[None, None, None, :] == 0) & (slot_ids[None, None, :, None] == 0)
    filled = jnp.where(anchor, 1, filled)
    result = jnp.where(live_slot[..., None], filled, 0)
    return result.reshape((N_DP, N_SPACE * BLK_DEV, VOX)).astype(jnp.int32)


def draw_rulebook(key, part):
    counts = live_counts(key)
    slot_ids = jnp.arange(BLK_DEV, dtype=jnp.int32)
    live_slot = slot_ids[None, None, :] < counts[:, :, None]
    picks = jax.random.randint(jax.random.fold_in(key, 31), (N_DP, N_SPACE, BLK_DEV, 27), 0, 2 * BLK_DEV + 1)
    device_ids = jnp.arange(N_SPACE, dtype=jnp.int32)[None, :, None, None]
    absent = 3 * BLK_DEV
    middle = jnp.where(picks < BLK_DEV, picks, jnp.where(picks < 2 * BLK_DEV, picks - BLK_DEV, absent))
    lowest = jnp.where(picks < 2 * BLK_DEV, picks, absent)
    lowest = jnp.where((device_ids == 0) & (picks >= BLK_DEV), absent, lowest)
    highest = jnp.where(picks < BLK_DEV, picks, jnp.where(picks < 2 * BLK_DEV, picks + BLK_DEV, absent))
    highest = jnp.where((device_ids == N_SPACE - 1) & (picks >= BLK_DEV), absent, highest)
    offsets = jnp.arange(27, dtype=jnp.int32)[None, None, None, :]
    depth = offsets % 3
    rule_rows = jnp.where(depth == 0, lowest, jnp.where(depth == 1, middle, highest))
    rule_rows = jnp.where(offsets == 13, slot_ids[None, None, :, None], rule_rows)
    rule_rows = jnp.where(live_slot[..., None] | (offsets == 13), rule_rows, absent)
    return rule_rows.reshape((N_DP, N_SPACE * BLK_DEV, 27)).astype(jnp.int32)


def plant(entries, stream_key, low, top_value):
    longest = entries.shape.index(max(entries.shape))
    spots = []
    for shift in (0, 1):
        where = [jax.random.randint(jax.random.fold_in(stream_key, axis), (), 0, length) for axis, length in enumerate(entries.shape)]
        where[longest] = (where[longest] + shift) % entries.shape[longest]
        spots.append(tuple(where))
    return entries.at[spots[0]].set(low).at[spots[1]].set(top_value)


def shard_levels(rng, shape, split, least, top_value):
    def one(axis_at, blocks):
        heights = jax.random.uniform(jax.random.fold_in(jax.random.fold_in(rng, 6), axis_at), (blocks,), jnp.float32, least / len(split), top_value / len(split))
        return jnp.repeat(jnp.exp(heights), shape[axis_at] // blocks).reshape((-1,) + (1,) * (len(shape) - axis_at - 1))

    factor_of = one(*split[0])
    for cut in split[1:]:
        factor_of = factor_of * one(*cut)
    return factor_of


def bell_draw(own_key, dims, deviation, limit, cuts=(), held_as=jnp.bfloat16):
    factor_of = shard_levels(own_key, dims, cuts, -0.22, 0.18) if cuts else 1.0
    entries = jax.random.normal(own_key, dims, jnp.float32) * deviation * factor_of
    return jnp.minimum(jnp.maximum(entries, -limit), limit).astype(held_as)


def setup_inputs(seed: int = 0) -> dict:
    key_list = jax.random.split(jax.random.key(seed), 8)
    return {
        "features": bell_draw(key_list[0], (N_DP, SLOTS, VOX, C), 1.0, 6.0, ((0, 4), (1, 8))),
        "occupancy": draw_occupancy(jax.random.fold_in(key_list[7], 71), 0),
        "labels": plant(jax.random.randint(key_list[2], (N_DP, SLOTS, VOX), 0, CLASSES), jax.random.fold_in(key_list[2], 1), 0, CLASSES - 1).astype(jnp.int32),
        "rulebook": draw_rulebook(jax.random.fold_in(key_list[7], 71), 0),
        "filter_one": bell_draw(key_list[4], (27, C, C), (27 * C) ** -0.5, 0.109375),
        "filter_two": bell_draw(key_list[5], (27, C, C), (27 * C) ** -0.5, 0.109375),
        "head_weight": bell_draw(key_list[6], (C, CLASSES), 0.25, 1.5),
    }


def blocks_of(values):
    return values.reshape((values.shape[0], EDGE, EDGE, EDGE, values.shape[-1]))

def assemble(local_blocks, below_top, above_bottom, rule_rows):
    slot_count = local_blocks.shape[0]
    shape_full = local_blocks.shape
    layer_shape = (shape_full[1], shape_full[2], 1, shape_full[4])
    dtype_in = local_blocks.dtype
    centre = jnp.concatenate([local_blocks, jnp.zeros((2 * slot_count + 1,) + shape_full[1:], dtype_in)], axis=0)
    low_table = jnp.concatenate([local_blocks[:, :, :, EDGE - 1:EDGE], below_top, jnp.zeros((slot_count + 1,) + layer_shape, dtype_in)], axis=0)
    high_table = jnp.concatenate([local_blocks[:, :, :, 0:1], jnp.zeros((slot_count,) + layer_shape, dtype_in), above_bottom, jnp.zeros((1,) + layer_shape, dtype_in)], axis=0)
    tables = (low_table, centre, high_table)
    bounds = ((EDGE - 1, EDGE), (0, EDGE), (0, 1))
    planes = []
    for step_x in range(3):
        columns = []
        for step_y in range(3):
            pieces = []
            for step_z in range(3):
                table = tables[step_z][:, bounds[step_x][0]:bounds[step_x][1], bounds[step_y][0]:bounds[step_y][1]]
                pieces.append(jnp.take(table, rule_rows[:, (step_x * 3 + step_y) * 3 + step_z], axis=0))
            columns.append(jnp.concatenate(pieces, axis=3))
        planes.append(jnp.concatenate(columns, axis=2))
    return jnp.concatenate(planes, axis=1)

def windows(padded, step_x, step_y, step_z):
    window = padded[:, step_x:step_x + EDGE, step_y:step_y + EDGE, step_z:step_z + EDGE]
    return window.reshape((padded.shape[0] * EDGE ** 3, padded.shape[-1]))

def forward_conv(padded, weights):
    summed = jnp.zeros((padded.shape[0] * EDGE ** 3, weights.shape[2]), jnp.float32)
    for offset in range(27):
        window = windows(padded, offset // 9, offset // 3 % 3, offset % 3)
        summed = summed + jnp.dot(window, weights[offset], preferred_element_type=jnp.float32)
    return summed

def transpose_conv(padded, weights):
    summed = jnp.zeros((padded.shape[0] * EDGE ** 3, weights.shape[1]), jnp.float32)
    for offset in range(27):
        window = windows(padded, 2 - offset // 9, 2 - offset // 3 % 3, 2 - offset % 3)
        summed = summed + jnp.dot(window, weights[offset].T, preferred_element_type=jnp.float32)
    return summed

def filter_grad(padded, cotangent):
    terms = []
    for offset in range(27):
        window = windows(padded, offset // 9, offset // 3 % 3, offset % 3)
        terms.append(lax.dot_general(window, cotangent, (((0,), (0,)), ((), ())), preferred_element_type=jnp.float32))
    return jnp.stack(terms)

def silu_slope(pre_act):
    sigmoid = jax.nn.sigmoid(pre_act)
    return sigmoid * (1.0 + pre_act * (1.0 - sigmoid))

def head_part(act_two, pre_two, occupied, label_ids, head_weight):
    mask_col = occupied.astype(jnp.float32)[:, None]
    logits = jnp.dot(act_two, head_weight, preferred_element_type=jnp.float32)
    classes = jnp.arange(head_weight.shape[1], dtype=jnp.int32)
    onehot = (label_ids[:, None] == classes[None, :]).astype(jnp.float32)
    total_log = jax.nn.logsumexp(logits, axis=1, keepdims=True)
    losses = jnp.sum((total_log - logits) * onehot * mask_col)
    dlogits = (jnp.exp(logits - total_log) - onehot) * mask_col
    head_term = lax.dot_general(act_two.astype(jnp.float32), dlogits, (((0,), (0,)), ((), ())), precision=lax.Precision.HIGHEST, preferred_element_type=jnp.float32)
    back_two = jnp.dot(dlogits, head_weight.astype(jnp.float32).T, precision=lax.Precision.HIGHEST, preferred_element_type=jnp.float32)
    grad_two = (back_two * silu_slope(pre_two) * mask_col).astype(jnp.bfloat16)
    return (grad_two, head_term, losses, jnp.sum(mask_col))

def reference(features, occupancy, labels, rulebook, filter_one, filter_two, head_weight):
    crop_count = features.shape[0]
    device_count = crop_count * N_SPACE
    channels = features.shape[-1]
    row_count = BLK_DEV * VOX

    def by_device(array):
        return array.reshape((device_count, BLK_DEV) + array.shape[2:])
    values = by_device(features)
    occupied = by_device(occupancy)
    rule_rows = by_device(rulebook)
    label_ids = by_device(labels).reshape((device_count, row_count))
    flat_mask = occupied.reshape((device_count, row_count))
    mask_cols = flat_mask.astype(jnp.float32)[:, :, None]

    def spread(blocks_all):
        layout = blocks_all.reshape((crop_count, N_SPACE) + blocks_all.shape[1:])
        zero_rows = jnp.zeros_like(layout[:, :1])
        from_below = jnp.concatenate([zero_rows, layout[:, :-1]], axis=1).reshape(blocks_all.shape)
        from_above = jnp.concatenate([layout[:, 1:], zero_rows], axis=1).reshape(blocks_all.shape)

        def build(entry):
            local_blocks = blocks_of(entry[0])
            return assemble(local_blocks, blocks_of(entry[1])[:, :, :, EDGE - 1:EDGE], blocks_of(entry[2])[:, :, :, 0:1], entry[3])
        return lax.map(build, (blocks_all, from_below, from_above, rule_rows))
    masked_in = values * occupied[..., None].astype(jnp.bfloat16)
    pad_in = spread(masked_in)
    pre_one = lax.map(partial(forward_conv, weights=filter_one), pad_in) * mask_cols
    act_one = jax.nn.silu(pre_one).astype(jnp.bfloat16)
    pad_act = spread(act_one.reshape(values.shape))
    pre_two = lax.map(partial(forward_conv, weights=filter_two), pad_act) * mask_cols
    act_two = jax.nn.silu(pre_two).astype(jnp.bfloat16)

    def head_step(entry):
        return head_part(entry[0], entry[1], entry[2], entry[3], head_weight)
    grad_two, head_terms, losses, counted = lax.map(head_step, (act_two, pre_two, flat_mask, label_ids))
    pad_grad_two = spread(grad_two.reshape(values.shape))

    def accumulate(summed, entry):
        return (summed + filter_grad(entry[0], entry[1]), None)
    zero_filter = jnp.zeros((27, channels, channels), jnp.float32)
    sum_two = lax.scan(accumulate, zero_filter, (pad_act, grad_two))[0]
    back_one = lax.map(partial(transpose_conv, weights=filter_two), pad_grad_two)
    grad_one = (back_one * silu_slope(pre_one) * mask_cols).astype(jnp.bfloat16)
    sum_one = lax.scan(accumulate, zero_filter, (pad_in, grad_one))[0]
    pad_grad_one = spread(grad_one.reshape(values.shape))
    grad_in = (lax.map(partial(transpose_conv, weights=filter_one), pad_grad_one) * mask_cols).astype(jnp.bfloat16)
    scale = 1.0 / VOX
    return (sum_one * scale, sum_two * scale, lax.optimization_barrier(jnp.sum(head_terms, axis=0)) * scale, jnp.sum(losses) / jnp.sum(counted), grad_in.reshape(features.shape))
```

```python
import functools

import jax
import jax.numpy as jnp
from jax import lax
from jax.experimental import pallas as pl
from jax.experimental.pallas import tpu as pltpu
from jax.sharding import Mesh, PartitionSpec as P

EDGE = 8
VOX = 512
LANES = 128
TAPS = 9
SMALL = 8
F32 = jnp.float32
BF16 = jnp.bfloat16
PARAMS = pltpu.CompilerParams(vmem_limit_bytes=40 * 1024 * 1024)
VMEM = pl.BlockSpec(memory_space=pltpu.VMEM)
SMEM = pl.BlockSpec(memory_space=pltpu.SMEM)


def sds(shape, dtype):
    return jax.ShapeDtypeStruct(shape, dtype)


def contract(a, b, dim_a, dim_b):
    return lax.dot_general(a, b, (((dim_a,), (dim_b,)), ((), ())), preferred_element_type=F32)


def spread_layer(layer):
    return jnp.broadcast_to(layer.astype(F32).reshape(64, 1, LANES), (64, EDGE, LANES))


def build_windows(block, recv_a, recv_b, rule_ref, parity_ref, out_ref):
    cells = block.reshape(64, EDGE, LANES)
    even = parity_ref[0] == 0
    got_a, got_b = recv_a.astype(F32), recv_b.astype(F32)
    below = jnp.where(even, got_b, got_a)
    above = jnp.where(even, got_a, got_b)
    depth = lax.broadcasted_iota(jnp.int32, (1, EDGE, LANES), 1)

    def flag(i, j, k, wanted):
        return jnp.where(rule_ref[9 * i + 3 * j + k] == wanted, 1.0, 0.0).astype(F32)

    for k in range(3):
        if k == 1:
            own, other = cells, None
        elif k == 0:
            own, other = pltpu.roll(cells, 1, 1), spread_layer(below)
        else:
            own, other = pltpu.roll(cells, EDGE - 1, 1), spread_layer(above)
        own = own.reshape(EDGE, EDGE, EDGE, LANES)
        if other is not None:
            other = other.reshape(EDGE, EDGE, EDGE, LANES)

        def region(i, j):
            xs = {0: slice(7, 8), 1: slice(0, 8), 2: slice(0, 1)}[i]
            ys = {0: slice(7, 8), 1: slice(0, 8), 2: slice(0, 1)}[j]
            inner = flag(i, j, 1, 0)
            if k == 1:
                return own[xs, ys] * inner
            edge = depth == (0 if k == 0 else EDGE - 1)
            keep = jnp.where(edge, flag(i, j, k, 0), inner)
            take = jnp.where(edge, flag(i, j, k, 1 if k == 0 else 2), 0.0)
            return own[xs, ys] * keep[None] + other[xs, ys] * take[None]

        columns = [jnp.concatenate([region(i, j) for i in range(3)], axis=0).astype(F32) for j in range(3)]
        for j in range(3):
            if j == 0:
                padded = jnp.concatenate([columns[0], columns[1][:, :7]], axis=1)
            elif j == 1:
                padded = columns[1]
            else:
                padded = jnp.concatenate([columns[1][:, 1:], columns[2]], axis=1)
            lane = (3 * j + k) * LANES
            out_ref[:, lane : lane + LANES] = padded.reshape(640, LANES).astype(BF16)


def put_layers(block, parity_ref, send_a_ref, send_b_ref):
    cells = block.reshape(64, EDGE, LANES)
    top, bottom = cells[:, EDGE - 1, :], cells[:, 0, :]
    even = parity_ref[0] == 0
    send_a_ref[...] = jnp.where(even, top, bottom).astype(BF16)
    send_b_ref[...] = jnp.where(even, bottom, top).astype(BF16)


def forward_sum(win_ref, filt_ref):
    total = None
    for i in range(3):
        filt = filt_ref[TAPS * i : TAPS * (i + 1)].reshape(TAPS * LANES, LANES)
        term = jnp.dot(win_ref[64 * i : 64 * i + VOX, :], filt, preferred_element_type=F32)
        total = term if total is None else total + term
    return total


def backward_sum(win_ref, filt_ref):
    total = None
    for i in range(3):
        filt = jnp.concatenate([filt_ref[26 - TAPS * i - t] for t in range(TAPS)], axis=1)
        term = contract(win_ref[64 * i : 64 * i + VOX, :], filt, 1, 1)
        total = term if total is None else total + term
    return total


def filter_terms(win_ref, grad, wide_ref, out_ref):
    wide_ref[...] = jnp.zeros_like(wide_ref)
    for i in range(3):
        wide_ref[64 * i : 64 * i + VOX, LANES * i : LANES * (i + 1)] = grad
    for t in range(TAPS):
        term = contract(win_ref[:, LANES * t : LANES * (t + 1)], wide_ref[...], 0, 0)
        for i in range(3):
            out_ref[TAPS * i + t] = term[:, LANES * i : LANES * (i + 1)].astype(BF16)


def silu_parts(pre):
    sigmoid = 1.0 / (1.0 + jnp.exp(-pre))
    return pre * sigmoid, sigmoid * (1.0 + pre * (1.0 - sigmoid))


def first_kernel(parity, feat, occ, labels, masked, mask, onehot, send_a, send_b):
    rows = lax.broadcasted_iota(jnp.int32, (SMALL, VOX), 0)
    occ_rows = jnp.where(rows == 0, jnp.broadcast_to(occ[...], (SMALL, VOX)), 0).astype(F32).astype(BF16)
    hot_rows = jnp.where(rows == jnp.broadcast_to(labels[...], (SMALL, VOX)), 1.0, 0.0).astype(BF16)
    row = lax.broadcasted_iota(jnp.int32, (SMALL, LANES), 0)
    lane = lax.broadcasted_iota(jnp.int32, (SMALL, LANES), 1)
    first = jnp.where(row == 0, 1.0, 0.0).astype(BF16)
    unit = jnp.where(row == lane, 1.0, 0.0).astype(BF16)
    filled = contract(occ_rows, first, 0, 0)
    mask[...] = filled
    onehot[...] = contract(hot_rows, unit, 0, 0)
    block = feat[...].astype(F32) * filled
    masked[...] = block.astype(BF16)
    put_layers(block, parity, send_a, send_b)


def one_kernel(rule, parity, masked, recv_a, recv_b, filt, mask, win, act, pre, send_a, send_b):
    build_windows(masked[...].astype(F32), recv_a[...], recv_b[...], rule, parity, win)
    total = forward_sum(win, filt) * mask[...]
    pre[...] = total
    acted, _ = silu_parts(total)
    act[...] = acted.astype(BF16)
    put_layers(acted.astype(BF16).astype(F32), parity, send_a, send_b)


def two_kernel(classes, rule, parity, act_one, recv_a, recv_b, filt, mask, onehot, head, win, grad, small, send_a, send_b):
    build_windows(act_one[...].astype(F32), recv_a[...], recv_b[...], rule, parity, win)
    filled = mask[...]
    pre = forward_sum(win, filt) * filled
    acted, slope = silu_parts(pre)
    acted = acted.astype(BF16)
    lane = lax.broadcasted_iota(jnp.int32, (VOX, LANES), 1)
    logits = contract(acted, head[...], 1, 1)
    known = lane < classes
    top = jnp.max(jnp.where(known, logits, -jnp.inf), axis=1, keepdims=True)
    powers = jnp.where(known, jnp.exp(jnp.where(known, logits - top, 0.0)), 0.0)
    total_log = top + jnp.log(jnp.sum(powers, axis=1, keepdims=True))
    hot = onehot[...]
    chances = jnp.where(known, jnp.exp(jnp.where(known, logits - total_log, 0.0)), 0.0)
    dlogits = (chances - hot) * filled
    high = dlogits.astype(BF16)
    low = (dlogits - high.astype(F32)).astype(BF16)
    back = jnp.dot(high, head[...], preferred_element_type=F32) + jnp.dot(low, head[...], preferred_element_type=F32)
    out = (back * slope * filled).astype(BF16)
    grad[...] = out
    put_layers(out.astype(F32), parity, send_a, send_b)
    head_rows = (contract(high, acted, 0, 0) + contract(low, acted, 0, 0))[:SMALL]
    losses = jnp.sum((total_log - logits) * hot * filled, axis=0, keepdims=True)
    counted = jnp.sum(filled, axis=0, keepdims=True)
    tail = jnp.where(lane[:1] < classes, losses, jnp.where(lane[:1] == classes, counted, 0.0))
    row = lax.broadcasted_iota(jnp.int32, (SMALL, LANES), 0)
    values = jnp.where(row < classes, head_rows, jnp.where(row == classes, tail, 0.0))
    small[...] = values


def terms_kernel(win, grad, out, wide):
    filter_terms(win, grad[...], wide, out)


def three_kernel(rule, parity, grad_two, recv_a, recv_b, filt, mask, pre, win_one, grad_one, terms, send_a, send_b, win, wide):
    build_windows(grad_two[...].astype(F32), recv_a[...], recv_b[...], rule, parity, win)
    _, slope = silu_parts(pre[...])
    out = (backward_sum(win, filt) * slope * mask[...]).astype(BF16)
    grad_one[...] = out
    put_layers(out.astype(F32), parity, send_a, send_b)
    filter_terms(win_one, out, wide, terms)


def four_kernel(rule, parity, grad_one, recv_a, recv_b, filt, mask, out, win):
    build_windows(grad_one[...].astype(F32), recv_a[...], recv_b[...], rule, parity, win)
    out[...] = (backward_sum(win, filt) * mask[...]).astype(BF16)


def call(kernel, outs, specs, scratch=(), flops=0):
    return pl.pallas_call(
        kernel,
        out_shape=outs,
        in_specs=specs,
        out_specs=jax.tree.map(lambda _: VMEM, outs),
        scratch_shapes=list(scratch),
        compiler_params=PARAMS,
        cost_estimate=pl.CostEstimate(flops=flops, bytes_accessed=4_000_000, transcendentals=0),
    )


BLOCK = sds((VOX, LANES), BF16)
WIDE_BLOCK = sds((VOX, LANES), F32)
LAYER = sds((64, LANES), BF16)
WINDOWS = sds((640, TAPS * LANES), BF16)
TERMS = sds((27, LANES, LANES), BF16)
WIN_SCRATCH = pltpu.VMEM((640, TAPS * LANES), BF16)
WIDE_SCRATCH = pltpu.VMEM((640, 3 * LANES), BF16)
CONV = 2 * 27 * VOX * LANES * LANES


def swap_layers(send_a, send_b):
    length = lax.axis_size("space")
    pairs_a = [(i, i ^ 1) for i in range(length)]
    pairs_b = [(i, (i + 1) % length if i % 2 else (i - 1) % length) for i in range(length)]
    return lax.ppermute(send_a, "space", pairs_a), lax.ppermute(send_b, "space", pairs_b)


def core_swap(value):
    return lax.ppermute(value, "core", [(0, 1), (1, 0)])


def split_pair(value):
    high = value.astype(BF16)
    return jnp.concatenate([high, (value - high.astype(F32)).astype(BF16)], axis=0)


def join_pair(pair):
    half = pair.shape[0] // 2
    return pair[:half].astype(F32) + pair[half:].astype(F32)


def pair_kernel(rows, peers, mine, other, small_mine, small_other, out):
    small = join_pair(small_mine[...]) + join_pair(small_other[...])
    tail = split_pair(small)
    total = mine[...].reshape(27 * LANES, LANES).astype(F32) + other[...].reshape(27 * LANES, LANES).astype(F32)
    total = total.astype(BF16)
    spare = rows * peers - 27 * LANES
    if spare:
        total = jnp.concatenate([total, jnp.zeros((spare, LANES), BF16)], axis=0)
    for p in range(peers):
        out[p] = jnp.concatenate([total[p * rows : (p + 1) * rows], tail], axis=0)


def sum_kernel(rows, peers, parts, out, small):
    total = parts[0].astype(F32)
    half = SMALL // 2
    for p in range(1, peers):
        total = total + parts[p].astype(F32)
    result = total[:rows].astype(BF16)
    for p in range(peers):
        out[p] = result
    tail = total[rows:]
    small[...] = jnp.concatenate([tail[:half] + tail[half:], jnp.zeros((half, LANES), F32)], axis=0)


def local(classes, features, occupancy, labels, rulebook, filter_one, filter_two, head_weight):
    parity = (lax.axis_index("space") % 2).reshape(1).astype(jnp.int32)
    rule = rulebook.reshape(27)
    head = jnp.zeros((LANES, LANES), BF16).at[:classes].set(head_weight.T)
    masked, mask, onehot, a, b = call(
        first_kernel, (BLOCK, WIDE_BLOCK, WIDE_BLOCK, LAYER, LAYER), [SMEM] + [VMEM] * 3
    )(parity, features.reshape(VOX, LANES), occupancy.reshape(1, VOX), labels.reshape(1, VOX))
    a, b = swap_layers(a, b)
    win_one, act_one, pre_one, c, d = call(
        one_kernel, (WINDOWS, BLOCK, WIDE_BLOCK, LAYER, LAYER), [SMEM] * 2 + [VMEM] * 5, flops=CONV
    )(rule, parity, masked, a, b, filter_one, mask)
    c, d = swap_layers(c, d)
    win_two, grad_two, small, e, f = call(
        functools.partial(two_kernel, classes),
        (WINDOWS, BLOCK, sds((SMALL, LANES), F32), LAYER, LAYER),
        [SMEM] * 2 + [VMEM] * 7,
        flops=CONV,
    )(rule, parity, act_one, c, d, filter_two, mask, onehot, head)
    e, f = swap_layers(e, f)
    terms_two = call(terms_kernel, TERMS, [VMEM] * 2, [WIDE_SCRATCH], flops=CONV)(win_two, grad_two)
    grad_one, terms_one, g, h = call(
        three_kernel, (BLOCK, TERMS, LAYER, LAYER), [SMEM] * 2 + [VMEM] * 7, [WIN_SCRATCH, WIDE_SCRATCH], flops=2 * CONV
    )(rule, parity, grad_two, e, f, filter_two, mask, pre_one, win_one)
    g, h = swap_layers(g, h)
    grad_in = call(four_kernel, BLOCK, [SMEM] * 2 + [VMEM] * 5, [WIN_SCRATCH], flops=CONV)(
        rule, parity, grad_one, g, h, filter_one, mask
    )

    core = lax.axis_index("core")
    peers = lax.axis_size("space") * lax.axis_size("x")
    rows = -(-27 * LANES // (peers * SMALL)) * SMALL
    small_pair = split_pair(small[: SMALL // 2])
    mine = jnp.where(core == 0, terms_one, terms_two)
    away = jnp.where(core == 0, terms_two, terms_one)
    other, small_other = core_swap(away), core_swap(small_pair)
    chunks = call(
        functools.partial(pair_kernel, rows, peers), sds((peers, rows + SMALL, LANES), BF16), [VMEM] * 4
    )(mine, other, small_pair, small_other)
    parts = lax.all_to_all(chunks, ("space", "x"), 0, 0, tiled=True)
    copies, sums = call(
        functools.partial(sum_kernel, rows, peers),
        (sds((peers, rows, LANES), BF16), sds((SMALL, LANES), F32)),
        [VMEM],
    )(parts)
    whole = lax.all_to_all(copies, ("space", "x"), 0, 0, tiled=True)
    whole = whole.reshape(peers * rows, LANES)[: 27 * LANES].reshape(27, LANES, LANES)
    whole_other = core_swap(whole)
    scale = 1.0 / VOX
    sum_one = jnp.where(core == 0, whole, whole_other).astype(F32) * scale
    sum_two = jnp.where(core == 0, whole_other, whole).astype(F32) * scale
    return (
        sum_one,
        sum_two,
        sums[:classes].T * scale,
        jnp.sum(sums[classes, :classes]) / sums[classes, classes],
        grad_in.reshape(features.shape),
    )


def solution(mesh):
    shape = mesh.devices.shape
    inner = Mesh(mesh.devices.reshape(shape[0], shape[1] // 2, 2), ("space", "x", "core"))
    parts = ("x", "core")
    placed = (
        P(parts, "space", None, None),
        P(parts, "space", None),
        P(parts, "space", None),
        P(parts, "space", None),
        P(),
        P(),
        P(),
    )

    def whole(features, occupancy, labels, rulebook, filter_one, filter_two, head_weight):
        step = jax.shard_map(
            functools.partial(local, head_weight.shape[1]),
            mesh=inner,
            in_specs=placed,
            out_specs=(P(), P(), P(), P(), P(parts, "space", None, None)),
            check_vma=False,
        )
        return step(features, occupancy, labels, rulebook, filter_one, filter_two, head_weight)

    return whole
```

```python
import functools

import jax
import jax.numpy as jnp
from jax import lax
from jax.experimental import pallas as pl
from jax.experimental.pallas import tpu as pltpu
from jax.sharding import Mesh, PartitionSpec as P

EDGE = 8
VOX = 512
LANES = 128
TAPS = 9
SMALL = 8
SPACE = ("far", "near")
F32 = jnp.float32
BF16 = jnp.bfloat16
PARAMS = pltpu.CompilerParams(vmem_limit_bytes=40 * 1024 * 1024)
VMEM = pl.BlockSpec(memory_space=pltpu.VMEM)
ANY = pl.BlockSpec(memory_space=pl.ANY)
SMEM = pl.BlockSpec(memory_space=pltpu.SMEM)


def sds(shape, dtype):
    return jax.ShapeDtypeStruct(shape, dtype)


def contract(a, b, dim_a, dim_b):
    return lax.dot_general(a, b, (((dim_a,), (dim_b,)), ((), ())), preferred_element_type=F32)


def spread_layer(layer):
    return jnp.broadcast_to(layer.astype(F32).reshape(64, 1, LANES), (64, EDGE, LANES))


def build_windows(block, recv_a, recv_b, rule_ref, parity_ref, out_ref):
    cells = block.reshape(64, EDGE, LANES)
    even = parity_ref[0] == 0
    got_a, got_b = recv_a.astype(F32), recv_b.astype(F32)
    below = jnp.where(even, got_b, got_a)
    above = jnp.where(even, got_a, got_b)
    depth = lax.broadcasted_iota(jnp.int32, (1, EDGE, LANES), 1)

    def flag(i, j, k, wanted):
        return jnp.where(rule_ref[9 * i + 3 * j + k] == wanted, 1.0, 0.0).astype(F32)

    for k in range(3):
        if k == 1:
            own, other = cells, None
        elif k == 0:
            own, other = pltpu.roll(cells, 1, 1), spread_layer(below)
        else:
            own, other = pltpu.roll(cells, EDGE - 1, 1), spread_layer(above)
        own = own.reshape(EDGE, EDGE, EDGE, LANES)
        if other is not None:
            other = other.reshape(EDGE, EDGE, EDGE, LANES)

        def region(i, j):
            xs = {0: slice(7, 8), 1: slice(0, 8), 2: slice(0, 1)}[i]
            ys = {0: slice(7, 8), 1: slice(0, 8), 2: slice(0, 1)}[j]
            inner = flag(i, j, 1, 0)
            if k == 1:
                return own[xs, ys] * inner
            edge = depth == (0 if k == 0 else EDGE - 1)
            keep = jnp.where(edge, flag(i, j, k, 0), inner)
            take = jnp.where(edge, flag(i, j, k, 1 if k == 0 else 2), 0.0)
            return own[xs, ys] * keep[None] + other[xs, ys] * take[None]

        columns = [jnp.concatenate([region(i, j) for i in range(3)], axis=0).astype(F32) for j in range(3)]
        for j in range(3):
            if j == 0:
                padded = jnp.concatenate([columns[0], columns[1][:, :7]], axis=1)
            elif j == 1:
                padded = columns[1]
            else:
                padded = jnp.concatenate([columns[1][:, 1:], columns[2]], axis=1)
            lane = (3 * j + k) * LANES
            out_ref[:, lane : lane + LANES] = padded.reshape(640, LANES).astype(BF16)


def put_layers(block, parity_ref, send_a_ref, send_b_ref):
    cells = block.reshape(64, EDGE, LANES)
    top, bottom = cells[:, EDGE - 1, :], cells[:, 0, :]
    even = parity_ref[0] == 0
    send_a_ref[...] = jnp.where(even, top, bottom).astype(BF16)
    send_b_ref[...] = jnp.where(even, bottom, top).astype(BF16)


def forward_sum(win_ref, filt_ref):
    total = None
    for i in range(3):
        filt = filt_ref[TAPS * i : TAPS * (i + 1)].reshape(TAPS * LANES, LANES)
        term = jnp.dot(win_ref[64 * i : 64 * i + VOX, :], filt, preferred_element_type=F32)
        total = term if total is None else total + term
    return total


def backward_sum(win_ref, filt_ref):
    total = None
    for i in range(3):
        filt = jnp.concatenate([filt_ref[26 - TAPS * i - t] for t in range(TAPS)], axis=1)
        term = contract(win_ref[64 * i : 64 * i + VOX, :], filt, 1, 1)
        total = term if total is None else total + term
    return total


def filter_terms(win_ref, grad, wide_ref, out_ref):
    wide_ref[...] = jnp.zeros_like(wide_ref)
    for i in range(3):
        wide_ref[64 * i : 64 * i + VOX, LANES * i : LANES * (i + 1)] = grad
    for t in range(TAPS):
        term = contract(win_ref[:, LANES * t : LANES * (t + 1)], wide_ref[...], 0, 0)
        for i in range(3):
            out_ref[TAPS * i + t] = term[:, LANES * i : LANES * (i + 1)].astype(BF16)


def silu_parts(pre):
    sigmoid = 1.0 / (1.0 + jnp.exp(-pre))
    return pre * sigmoid, sigmoid * (1.0 + pre * (1.0 - sigmoid))


def first_kernel(parity, feat, occ, labels, masked, mask, onehot, send_a, send_b):
    rows = lax.broadcasted_iota(jnp.int32, (SMALL, VOX), 0)
    occ_rows = jnp.where(rows == 0, jnp.broadcast_to(occ[...], (SMALL, VOX)), 0).astype(F32).astype(BF16)
    hot_rows = jnp.where(rows == jnp.broadcast_to(labels[...], (SMALL, VOX)), 1.0, 0.0).astype(BF16)
    row = lax.broadcasted_iota(jnp.int32, (SMALL, LANES), 0)
    lane = lax.broadcasted_iota(jnp.int32, (SMALL, LANES), 1)
    first = jnp.where(row == 0, 1.0, 0.0).astype(BF16)
    unit = jnp.where(row == lane, 1.0, 0.0).astype(BF16)
    filled = contract(occ_rows, first, 0, 0)
    mask[...] = filled
    onehot[...] = contract(hot_rows, unit, 0, 0)
    block = feat[...].astype(F32) * filled
    masked[...] = block.astype(BF16)
    put_layers(block, parity, send_a, send_b)


def one_kernel(rule, parity, masked, recv_a, recv_b, filt, mask, win, act, pre, send_a, send_b):
    build_windows(masked[...].astype(F32), recv_a[...], recv_b[...], rule, parity, win)
    total = forward_sum(win, filt) * mask[...]
    pre[...] = total
    acted, _ = silu_parts(total)
    act[...] = acted.astype(BF16)
    put_layers(acted.astype(BF16).astype(F32), parity, send_a, send_b)


def two_kernel(classes, rule, parity, act_one, recv_a, recv_b, filt, mask, onehot, head, win, grad, small, send_a, send_b):
    build_windows(act_one[...].astype(F32), recv_a[...], recv_b[...], rule, parity, win)
    filled = mask[...]
    pre = forward_sum(win, filt) * filled
    acted, slope = silu_parts(pre)
    acted = acted.astype(BF16)
    lane = lax.broadcasted_iota(jnp.int32, (VOX, LANES), 1)
    logits = contract(acted, head[...], 1, 1)
    known = lane < classes
    top = jnp.max(jnp.where(known, logits, -jnp.inf), axis=1, keepdims=True)
    powers = jnp.where(known, jnp.exp(jnp.where(known, logits - top, 0.0)), 0.0)
    total_log = top + jnp.log(jnp.sum(powers, axis=1, keepdims=True))
    hot = onehot[...]
    chances = jnp.where(known, jnp.exp(jnp.where(known, logits - total_log, 0.0)), 0.0)
    dlogits = (chances - hot) * filled
    high = dlogits.astype(BF16)
    low = (dlogits - high.astype(F32)).astype(BF16)
    back = jnp.dot(high, head[...], preferred_element_type=F32) + jnp.dot(low, head[...], preferred_element_type=F32)
    out = (back * slope * filled).astype(BF16)
    grad[...] = out
    put_layers(out.astype(F32), parity, send_a, send_b)
    head_rows = (contract(high, acted, 0, 0) + contract(low, acted, 0, 0))[:SMALL]
    losses = jnp.sum((total_log - logits) * hot * filled, axis=0, keepdims=True)
    counted = jnp.sum(filled, axis=0, keepdims=True)
    tail = jnp.where(lane[:1] < classes, losses, jnp.where(lane[:1] == classes, counted, 0.0))
    row = lax.broadcasted_iota(jnp.int32, (SMALL, LANES), 0)
    values = jnp.where(row < classes, head_rows, jnp.where(row == classes, tail, 0.0))
    small[...] = values


def terms_kernel(win, grad, out, wide):
    filter_terms(win, grad[...], wide, out)


def three_kernel(rule, parity, grad_two, recv_a, recv_b, filt, mask, pre, win_one, grad_one, terms, send_a, send_b, win, wide):
    build_windows(grad_two[...].astype(F32), recv_a[...], recv_b[...], rule, parity, win)
    _, slope = silu_parts(pre[...])
    out = (backward_sum(win, filt) * slope * mask[...]).astype(BF16)
    grad_one[...] = out
    put_layers(out.astype(F32), parity, send_a, send_b)
    filter_terms(win_one, out, wide, terms)


def four_kernel(rule, parity, grad_one, recv_a, recv_b, filt, mask, out, win):
    build_windows(grad_one[...].astype(F32), recv_a[...], recv_b[...], rule, parity, win)
    out[...] = (backward_sum(win, filt) * mask[...]).astype(BF16)


def call(kernel, outs, specs, scratch=(), flops=0):
    return pl.pallas_call(
        kernel,
        out_shape=outs,
        in_specs=specs,
        out_specs=jax.tree.map(lambda _: VMEM, outs),
        scratch_shapes=list(scratch),
        compiler_params=PARAMS,
        cost_estimate=pl.CostEstimate(flops=flops, bytes_accessed=4_000_000, transcendentals=0),
    )


BLOCK = sds((VOX, LANES), BF16)
WIDE_BLOCK = sds((VOX, LANES), F32)
LAYER = sds((64, LANES), BF16)
WINDOWS = sds((640, TAPS * LANES), BF16)
TERMS = sds((27, LANES, LANES), BF16)
WIN_SCRATCH = pltpu.VMEM((640, TAPS * LANES), BF16)
WIDE_SCRATCH = pltpu.VMEM((640, 3 * LANES), BF16)
CONV = 2 * 27 * VOX * LANES * LANES


def swap_layers(send_a, send_b):
    length = lax.axis_size(SPACE)
    pairs_a = [(i, i ^ 1) for i in range(length)]
    pairs_b = [(i, (i + 1) % length if i % 2 else (i - 1) % length) for i in range(length)]
    return lax.ppermute(send_a, SPACE, pairs_a), lax.ppermute(send_b, SPACE, pairs_b)


def far_swap(value):
    return lax.ppermute(value, "far", [(0, 1), (1, 0)])


def core_swap(value):
    return lax.ppermute(value, "core", [(0, 1), (1, 0)])


def split_pair(value):
    high = value.astype(BF16).astype(F32)
    return jnp.concatenate([high, value - high], axis=0)


def join_pair(pair):
    return pair[: SMALL // 2] + pair[SMALL // 2 : SMALL]


def pair_kernel(rows, peers, mine, other, small_mine, small_other, out):
    small = join_pair(small_mine[...].astype(F32)) + join_pair(small_other[...].astype(F32))
    tail = jnp.concatenate([split_pair(small), jnp.zeros((SMALL, LANES), F32)], axis=0)
    total = mine[...].reshape(27 * LANES, LANES).astype(F32) + other[...].reshape(27 * LANES, LANES).astype(F32)
    spare = rows * peers - 27 * LANES
    if spare:
        total = jnp.concatenate([total, jnp.zeros((spare, LANES), F32)], axis=0)
    for p in range(peers):
        out[p] = jnp.concatenate([total[p * rows : (p + 1) * rows], tail], axis=0).astype(BF16)


def half_kernel(rows, peers, far, parts, later_a, later_b, keep, away):
    total = parts[0].astype(F32)
    for p in range(1, peers):
        total = total + parts[p].astype(F32)
    half = rows // 2
    near_part, far_part = total[:half], total[half:rows]
    tail = split_pair(join_pair(total[rows : rows + SMALL])).astype(BF16).astype(F32)
    low = far[0] == 0
    keep[...] = jnp.concatenate([jnp.where(low, near_part, far_part), tail], axis=0)
    away[...] = jnp.concatenate([jnp.where(low, far_part, near_part), tail], axis=0).astype(BF16)


def whole_kernel(half, keep, recv, out, small):
    got = recv[...].astype(F32)
    out[...] = (keep[:half] + got[:half]).astype(BF16)
    tail = join_pair(keep[half:]) + join_pair(got[half:])
    small[...] = jnp.concatenate([tail, jnp.zeros_like(tail)], axis=0)


def copies_kernel(peers, far, mine, other, later, out):
    low = far[0] == 0
    a, b = mine[...].astype(F32), other[...].astype(F32)
    both = jnp.concatenate([jnp.where(low, a, b), jnp.where(low, b, a)], axis=0).astype(BF16)
    for p in range(peers):
        out[p] = both


def local(classes, features, occupancy, labels, rulebook, filter_one, filter_two, head_weight):
    parity = (lax.axis_index(SPACE) % 2).reshape(1).astype(jnp.int32)
    rule = rulebook.reshape(27)
    head = jnp.zeros((LANES, LANES), BF16).at[:classes].set(head_weight.T)
    masked, mask, onehot, a, b = call(
        first_kernel, (BLOCK, WIDE_BLOCK, WIDE_BLOCK, LAYER, LAYER), [SMEM] + [VMEM] * 3
    )(parity, features.reshape(VOX, LANES), occupancy.reshape(1, VOX), labels.reshape(1, VOX))
    a, b = swap_layers(a, b)
    win_one, act_one, pre_one, c, d = call(
        one_kernel, (WINDOWS, BLOCK, WIDE_BLOCK, LAYER, LAYER), [SMEM] * 2 + [VMEM] * 5, flops=CONV
    )(rule, parity, masked, a, b, filter_one, mask)
    c, d = swap_layers(c, d)
    win_two, grad_two, small, e, f = call(
        functools.partial(two_kernel, classes),
        (WINDOWS, BLOCK, sds((SMALL, LANES), F32), LAYER, LAYER),
        [SMEM] * 2 + [VMEM] * 7,
        flops=CONV,
    )(rule, parity, act_one, c, d, filter_two, mask, onehot, head)
    e, f = swap_layers(e, f)
    terms_two = call(terms_kernel, TERMS, [VMEM] * 2, [WIDE_SCRATCH], flops=CONV)(win_two, grad_two)
    grad_one, terms_one, g, h = call(
        three_kernel, (BLOCK, TERMS, LAYER, LAYER), [SMEM] * 2 + [VMEM] * 7, [WIN_SCRATCH, WIDE_SCRATCH], flops=2 * CONV
    )(rule, parity, grad_two, e, f, filter_two, mask, pre_one, win_one)
    g, h = swap_layers(g, h)
    grad_in = call(four_kernel, BLOCK, [SMEM] * 2 + [VMEM] * 5, [WIN_SCRATCH], flops=CONV)(
        rule, parity, grad_one, g, h, filter_one, mask
    )

    core = lax.axis_index("core")
    far = lax.axis_index("far").reshape(1).astype(jnp.int32)
    peers = lax.axis_size("near") * lax.axis_size("x")
    half = -(-27 * LANES // (2 * peers * SMALL)) * SMALL
    rows = 2 * half
    small_pair = split_pair(small[: SMALL // 2]).astype(BF16)
    mine = jnp.where(core == 0, terms_one, terms_two)
    away = jnp.where(core == 0, terms_two, terms_one)
    other, small_other = core_swap(away), core_swap(small_pair)
    chunks = call(
        functools.partial(pair_kernel, rows, peers), sds((peers, rows + 2 * SMALL, LANES), BF16), [VMEM] * 4
    )(mine, other, small_pair, small_other)
    parts = lax.all_to_all(chunks, ("near", "x"), 0, 0, tiled=True)
    keep, away = call(
        functools.partial(half_kernel, rows, peers),
        (sds((half + SMALL, LANES), F32), sds((half + SMALL, LANES), BF16)),
        [SMEM, VMEM, ANY, ANY],
    )(far, parts, g, h)
    reduced, sums = call(
        functools.partial(whole_kernel, half), (sds((half, LANES), BF16), sds((SMALL, LANES), F32)), [VMEM] * 2
    )(keep, far_swap(away))
    copies = call(
        functools.partial(copies_kernel, peers), sds((peers, rows, LANES), BF16), [SMEM, VMEM, VMEM, ANY]
    )(far, reduced, far_swap(reduced), grad_in)
    whole = lax.all_to_all(copies, ("near", "x"), 0, 0, tiled=True)
    whole = whole.reshape(peers * rows, LANES)[: 27 * LANES].reshape(27, LANES, LANES)
    whole_other = core_swap(whole)
    scale = 1.0 / VOX
    sum_one = jnp.where(core == 0, whole, whole_other).astype(F32) * scale
    sum_two = jnp.where(core == 0, whole_other, whole).astype(F32) * scale
    return (
        sum_one,
        sum_two,
        sums[:classes].T * scale,
        jnp.sum(sums[classes, :classes]) / sums[classes, classes],
        grad_in.reshape(features.shape),
    )


def solution(mesh):
    shape = mesh.devices.shape
    inner = Mesh(mesh.devices.reshape(2, shape[0] // 2, shape[1] // 2, 2), ("far", "near", "x", "core"))
    parts = ("x", "core")
    placed = (
        P(parts, SPACE, None, None),
        P(parts, SPACE, None),
        P(parts, SPACE, None),
        P(parts, SPACE, None),
        P(),
        P(),
        P(),
    )

    def whole(features, occupancy, labels, rulebook, filter_one, filter_two, head_weight):
        step = jax.shard_map(
            functools.partial(local, head_weight.shape[1]),
            mesh=inner,
            in_specs=placed,
            out_specs=(P(), P(), P(), P(), P(parts, SPACE, None, None)),
            check_vma=False,
        )
        return step(features, occupancy, labels, rulebook, filter_one, filter_two, head_weight)

    return whole
```

```python
import functools

import jax
import jax.numpy as jnp
from jax import lax
from jax.experimental import pallas as pl
from jax.experimental.pallas import tpu as pltpu
from jax.sharding import Mesh, PartitionSpec as P

EDGE = 8
VOX = 512
LANES = 128
TAPS = 9
SMALL = 8
SPACE = ("far", "near")
F32 = jnp.float32
BF16 = jnp.bfloat16
PARAMS = pltpu.CompilerParams(vmem_limit_bytes=16 * 1024 * 1024)
VMEM = pl.BlockSpec(memory_space=pltpu.VMEM)
ANY = pl.BlockSpec(memory_space=pl.ANY)
SMEM = pl.BlockSpec(memory_space=pltpu.SMEM)


def sds(shape, dtype):
    return jax.ShapeDtypeStruct(shape, dtype)


def contract(a, b, dim_a, dim_b):
    return lax.dot_general(a, b, (((dim_a,), (dim_b,)), ((), ())), preferred_element_type=F32)


def spread_layer(layer):
    return jnp.broadcast_to(layer.astype(F32).reshape(64, 1, LANES), (64, EDGE, LANES))


def from_sides(parity_ref, recv_a, recv_b):
    even = parity_ref[0] == 0
    got_a, got_b = recv_a.astype(F32), recv_b.astype(F32)
    return jnp.where(even, got_b, got_a), jnp.where(even, got_a, got_b)


def build_windows(block, below, above, rule_ref, out_ref):
    cells = block.reshape(64, EDGE, LANES)
    depth = lax.broadcasted_iota(jnp.int32, (1, EDGE, LANES), 1)

    def flag(i, j, k, wanted):
        offset = 9 * i + 3 * j + k
        return jnp.where(rule_ref[offset : offset + 1, :] == wanted, 1.0, 0.0).reshape(1, 1, LANES)

    for k in range(3):
        if k == 1:
            own, other = cells, None
        elif k == 0:
            own, other = pltpu.roll(cells, 1, 1), spread_layer(below)
        else:
            own, other = pltpu.roll(cells, EDGE - 1, 1), spread_layer(above)
        own = own.reshape(EDGE, EDGE, EDGE, LANES)
        if other is not None:
            other = other.reshape(EDGE, EDGE, EDGE, LANES)

        def region(i, j):
            xs = {0: slice(7, 8), 1: slice(0, 8), 2: slice(0, 1)}[i]
            ys = {0: slice(7, 8), 1: slice(0, 8), 2: slice(0, 1)}[j]
            inner = flag(i, j, 1, 0)
            if k == 1:
                return own[xs, ys] * inner[None]
            edge = depth == (0 if k == 0 else EDGE - 1)
            keep = jnp.where(edge, flag(i, j, k, 0), inner)
            take = jnp.where(edge, flag(i, j, k, 1 if k == 0 else 2), 0.0)
            return own[xs, ys] * keep[None] + other[xs, ys] * take[None]

        columns = [jnp.concatenate([region(i, j) for i in range(3)], axis=0).astype(F32) for j in range(3)]
        for j in range(3):
            if j == 0:
                padded = jnp.concatenate([columns[0], columns[1][:, :7]], axis=1)
            elif j == 1:
                padded = columns[1]
            else:
                padded = jnp.concatenate([columns[1][:, 1:], columns[2]], axis=1)
            lane = (3 * j + k) * LANES
            out_ref[:, lane : lane + LANES] = padded.reshape(640, LANES).astype(BF16)


def put_sides(parity_ref, upward, downward, send_a_ref, send_b_ref):
    even = parity_ref[0] == 0
    send_a_ref[...] = jnp.where(even, upward, downward).astype(BF16)
    send_b_ref[...] = jnp.where(even, downward, upward).astype(BF16)


def layers_of(block):
    cells = block.reshape(64, EDGE, LANES)
    return lambda z: cells[:, z, :]


def put_layers(block, parity_ref, send_a_ref, send_b_ref):
    layer = layers_of(block)
    put_sides(parity_ref, layer(EDGE - 1), layer(0), send_a_ref, send_b_ref)


def layer_windows(side, mine, touching, rule, out_ref, row):
    near, behind, wrap = (part.reshape(EDGE, EDGE, LANES) for part in side)
    mine = mine.reshape(EDGE, EDGE, LANES)
    across = 2 if touching == EDGE - 1 else 0
    width = lax.broadcasted_iota(jnp.int32, (1, EDGE, LANES), 1)

    def flag(i, j, k, wanted):
        offset = 9 * i + 3 * j + k
        return jnp.where(rule[offset : offset + 1, :] == wanted, 1.0, 0.0).reshape(1, 1, LANES)

    for k in range(3):
        sources = [(near if k == 1 else behind, 1, 0)]
        if k == across:
            sources = [(wrap, k, 0), (mine, k, 2 if across == 2 else 1)]
        for j in range(3):
            base = first = last = None
            for layer, region, wanted in sources:
                turned = layer if j == 1 else pltpu.roll(layer, 1 if j == 0 else EDGE - 1, 1)

                def gate(i):
                    inner = flag(i, 1, region, wanted)
                    if j == 1:
                        return inner
                    return jnp.where(width == (0 if j == 0 else EDGE - 1), flag(i, j, region, wanted), inner)

                parts = turned * gate(1), turned[7:8] * gate(0), turned[0:1] * gate(2)
                if base is None:
                    base, first, last = parts
                else:
                    base, first, last = base + parts[0], first + parts[1], last + parts[2]
            for i in range(3):
                cells = base
                if i == 0:
                    cells = jnp.concatenate([first, base[:7]], axis=0)
                elif i == 2:
                    cells = jnp.concatenate([base[1:], last], axis=0)
                lane = (9 * i + 3 * j + k) * LANES
                out_ref[row : row + 64, lane : lane + LANES] = cells.reshape(64, LANES).astype(BF16)


def forward_sum(win_ref, filt_ref):
    total = None
    for i in range(3):
        filt = filt_ref[TAPS * i : TAPS * (i + 1)].reshape(TAPS * LANES, LANES)
        term = jnp.dot(win_ref[64 * i : 64 * i + VOX, :], filt, preferred_element_type=F32)
        total = term if total is None else total + term
    return total


def backward_sum(win_ref, filt_ref):
    total = None
    for i in range(3):
        filt = jnp.concatenate([filt_ref[26 - TAPS * i - t] for t in range(TAPS)], axis=1)
        term = contract(win_ref[64 * i : 64 * i + VOX, :], filt, 1, 1)
        total = term if total is None else total + term
    return total


def filter_terms(win_ref, grad, small_ref, wide_ref, out_ref):
    pair = split_pair(small_ref[: SMALL // 2])
    out_ref[27] = jnp.concatenate([pair, jnp.zeros((LANES - SMALL, LANES), F32)], axis=0).astype(BF16)
    wide_ref[...] = jnp.zeros_like(wide_ref)
    for i in range(3):
        wide_ref[64 * i : 64 * i + VOX, LANES * i : LANES * (i + 1)] = grad
    for t in range(TAPS):
        term = contract(win_ref[:, LANES * t : LANES * (t + 1)], wide_ref[...], 0, 0)
        for i in range(3):
            out_ref[TAPS * i + t] = term[:, LANES * i : LANES * (i + 1)].astype(BF16)


def silu_parts(pre):
    sigmoid = 1.0 / (1.0 + jnp.exp(-pre))
    return pre * sigmoid, sigmoid * (1.0 + pre * (1.0 - sigmoid))


def first_kernel(parity, feat_hbm, occ_hbm, rule_hbm, masked, mask, rule_rows, send_a, send_b, feat, occ, rule, sems):
    copies = [
        pltpu.make_async_copy(feat_hbm, feat, sems.at[0]),
        pltpu.make_async_copy(occ_hbm, occ, sems.at[1]),
        pltpu.make_async_copy(rule_hbm, rule, sems.at[2]),
    ]
    for copy in copies:
        copy.start()
    for copy in copies:
        copy.wait()
    rows = lax.broadcasted_iota(jnp.int32, (SMALL, VOX), 0)
    occ_rows = jnp.where(rows == 0, jnp.broadcast_to(occ[...], (SMALL, VOX)), 0).astype(F32).astype(BF16)
    row = lax.broadcasted_iota(jnp.int32, (SMALL, LANES), 0)
    first = jnp.where(row == 0, 1.0, 0.0).astype(BF16)
    filled = contract(occ_rows, first, 0, 0)
    mask[...] = filled
    block = feat[...].astype(F32) * filled
    masked[...] = block.astype(BF16)
    offsets = lax.broadcasted_iota(jnp.int32, (32, LANES), 0)
    found = jnp.zeros((32, LANES), jnp.int32)
    for o in range(27):
        found = jnp.where(offsets == o, rule[0, o], found)
    found = found.astype(F32)
    rule_rows[...] = found
    layer, held = layers_of(block), layers_of(filled)
    top = EDGE - 1
    upward = jnp.concatenate([layer(top), layer(top - 1), layer(0), held(top), found], axis=0)
    downward = jnp.concatenate([layer(0), layer(1), layer(top), held(0), found], axis=0)
    put_sides(parity, upward, downward, send_a, send_b)


def labels_kernel(labels, filt_in, onehot, filt):
    filt[...] = filt_in[...]
    rows = lax.broadcasted_iota(jnp.int32, (SMALL, VOX), 0)
    hot_rows = jnp.where(rows == jnp.broadcast_to(labels[...], (SMALL, VOX)), 1.0, 0.0).astype(BF16)
    row = lax.broadcasted_iota(jnp.int32, (SMALL, LANES), 0)
    lane = lax.broadcasted_iota(jnp.int32, (SMALL, LANES), 1)
    unit = jnp.where(row == lane, 1.0, 0.0).astype(BF16)
    onehot[...] = contract(hot_rows, unit, 0, 0)


def one_kernel(rule, parity, masked, recv_a, recv_b, filt, mask, act, act_below, act_above, pre, win, rim):
    below, above = from_sides(parity, recv_a[...], recv_b[...])
    block = masked[...].astype(F32)
    build_windows(block, below[:64], above[:64], rule, win)
    total = forward_sum(win, filt) * mask[...]
    pre[...] = total
    acted, _ = silu_parts(total)
    act[...] = acted.astype(BF16)
    layer = layers_of(block)
    for side, mine, touching, row in ((below, layer(0), EDGE - 1, 0), (above, layer(EDGE - 1), 0, 64)):
        parts = [side[at : at + 64] for at in (0, 64, 128)]
        layer_windows(parts, mine, touching, side[256:288], rim, row)
    total = None
    wide = TAPS * LANES
    for i in range(3):
        weights = filt[TAPS * i : TAPS * (i + 1)].reshape(wide, LANES)
        term = jnp.dot(rim[:, wide * i : wide * (i + 1)], weights, preferred_element_type=F32)
        total = term if total is None else total + term
    for side, row, out in ((below, 0, act_below), (above, 64, act_above)):
        acted, _ = silu_parts(total[row : row + 64] * side[192:256])
        out[...] = acted.astype(BF16)


def two_kernel(
    classes, rule, parity, act_one, act_below, act_above, filt, mask, onehot, head,
    win, grad, small, send_a, send_b,
):
    build_windows(act_one[...].astype(F32), act_below[...].astype(F32), act_above[...].astype(F32), rule, win)
    filled = mask[...]
    pre = forward_sum(win, filt) * filled
    acted, slope = silu_parts(pre)
    acted = acted.astype(BF16)
    lane = lax.broadcasted_iota(jnp.int32, (VOX, LANES), 1)
    logits = contract(acted, head[...], 1, 1)
    known = lane < classes
    top = jnp.max(jnp.where(known, logits, -jnp.inf), axis=1, keepdims=True)
    powers = jnp.where(known, jnp.exp(jnp.where(known, logits - top, 0.0)), 0.0)
    total_log = top + jnp.log(jnp.sum(powers, axis=1, keepdims=True))
    hot = onehot[...]
    chances = jnp.where(known, jnp.exp(jnp.where(known, logits - total_log, 0.0)), 0.0)
    dlogits = (chances - hot) * filled
    high = dlogits.astype(BF16)
    low = (dlogits - high.astype(F32)).astype(BF16)
    back = jnp.dot(high, head[...], preferred_element_type=F32) + jnp.dot(low, head[...], preferred_element_type=F32)
    out = (back * slope * filled).astype(BF16)
    grad[...] = out
    put_layers(out.astype(F32), parity, send_a, send_b)
    head_rows = (contract(high, acted, 0, 0) + contract(low, acted, 0, 0))[:SMALL]
    losses = jnp.sum((total_log - logits) * hot * filled, axis=0, keepdims=True)
    counted = jnp.sum(filled, axis=0, keepdims=True)
    tail = jnp.where(lane[:1] < classes, losses, jnp.where(lane[:1] == classes, counted, 0.0))
    row = lax.broadcasted_iota(jnp.int32, (SMALL, LANES), 0)
    values = jnp.where(row < classes, head_rows, jnp.where(row == classes, tail, 0.0))
    small[...] = values


def terms_kernel(rule, parity, masked, recv_a, recv_b, win_two, grad, small, out, win_one, wide):
    filter_terms(win_two, grad[...], small, wide, out)
    below, above = from_sides(parity, recv_a[...], recv_b[...])
    build_windows(masked[...].astype(F32), below[:64], above[:64], rule, win_one)


def three_kernel(
    rule, parity, grad_two, recv_a, recv_b, filt, mask, pre, win_one, small,
    grad_one, terms, send_a, send_b, win, wide,
):
    below, above = from_sides(parity, recv_a[...], recv_b[...])
    build_windows(grad_two[...].astype(F32), below, above, rule, win)
    _, slope = silu_parts(pre[...])
    out = (backward_sum(win, filt) * slope * mask[...]).astype(BF16)
    grad_one[...] = out
    put_layers(out.astype(F32), parity, send_a, send_b)
    filter_terms(win_one, out, small, wide, terms)


def four_kernel(rule, parity, grad_one, recv_a, recv_b, filt, mask, out, token, win):
    below, above = from_sides(parity, recv_a[...], recv_b[...])
    build_windows(grad_one[...].astype(F32), below, above, rule, win)
    total = backward_sum(win, filt) * mask[...]
    out[...] = total.astype(BF16)
    token[...] = total[:SMALL]


def call(kernel, outs, specs, scratch=(), flops=0, params=PARAMS):
    return pl.pallas_call(
        kernel,
        out_shape=outs,
        in_specs=specs,
        out_specs=jax.tree.map(lambda _: VMEM, outs),
        scratch_shapes=list(scratch),
        compiler_params=params,
        cost_estimate=pl.CostEstimate(flops=flops, bytes_accessed=4_000_000, transcendentals=0),
    )


BLOCK = sds((VOX, LANES), BF16)
WIDE_BLOCK = sds((VOX, LANES), F32)
LAYER = sds((64, LANES), BF16)
FILTER = sds((27, LANES, LANES), BF16)
SIDE = sds((288, LANES), BF16)
WINDOWS = sds((640, TAPS * LANES), BF16)
TERMS = sds((28, LANES, LANES), BF16)
WIN_SCRATCH = pltpu.VMEM((640, TAPS * LANES), BF16)
SEM = pltpu.SemaphoreType.DMA
WIDE_SCRATCH = pltpu.VMEM((640, 3 * LANES), BF16)
CONV = 2 * 27 * VOX * LANES * LANES


def swap_a(value):
    length = lax.axis_size(SPACE)
    return lax.ppermute(value, SPACE, [(i, i ^ 1) for i in range(length)])


def swap_b(value):
    length = lax.axis_size(SPACE)
    return lax.ppermute(value, SPACE, [(i, (i + 1) % length if i % 2 else (i - 1) % length) for i in range(length)])


def far_swap(value):
    return lax.ppermute(value, "far", [(0, 1), (1, 0)])


def core_swap(value):
    return lax.ppermute(value, "core", [(0, 1), (1, 0)])


def split_pair(value):
    high = value.astype(BF16).astype(F32)
    return jnp.concatenate([high, value - high], axis=0)


def join_pair(pair):
    return pair[: SMALL // 2] + pair[SMALL // 2 : SMALL]


def pair_kernel(rows, peers, core, one, two, other, out):
    small = join_pair(one[27].astype(F32)) + join_pair(other[27].astype(F32))
    tail = jnp.concatenate([split_pair(small), jnp.zeros((SMALL, LANES), F32)], axis=0)
    mine = jnp.where(core[0] == 0, one[:27], two[:27])
    total = mine.reshape(27 * LANES, LANES).astype(F32) + other[:27].reshape(27 * LANES, LANES).astype(F32)
    spare = rows * peers - 27 * LANES
    if spare:
        total = jnp.concatenate([total, jnp.zeros((spare, LANES), F32)], axis=0)
    for p in range(peers):
        out[p] = jnp.concatenate([total[p * rows : (p + 1) * rows], tail], axis=0).astype(BF16)


def half_kernel(rows, peers, parts, later_a, later_b, out):
    total = parts[0].astype(F32)
    for p in range(1, peers):
        total = total + parts[p].astype(F32)
    tail = split_pair(join_pair(total[rows : rows + SMALL]))
    out[...] = jnp.concatenate([total[:rows], tail, jnp.zeros((SMALL, LANES), F32)], axis=0).astype(BF16)


def copies_kernel(rows, peers, classes, mine, other, later, out, head, loss):
    a, b = mine[...].astype(F32), other[...].astype(F32)
    both = (a[:rows] + b[:rows]).astype(BF16)
    for p in range(peers):
        out[p] = both
    tail = join_pair(a[rows:]) + join_pair(b[rows:])
    head[...] = tail[:classes] * (1.0 / VOX)
    last = tail[classes : classes + 1]
    lane = lax.broadcasted_iota(jnp.int32, (1, LANES), 1)
    losses = jnp.sum(jnp.where(lane < classes, last, 0.0), axis=1, keepdims=True)
    counted = jnp.sum(jnp.where(lane == classes, last, 0.0), axis=1, keepdims=True)
    loss[...] = jnp.broadcast_to(losses / counted, (1, LANES))


def local(classes, features, occupancy, labels, rulebook, filter_one, filter_two, head_weight):
    parity = (lax.axis_index(SPACE) % 2).reshape(1).astype(jnp.int32)
    core = lax.axis_index("core").reshape(1).astype(jnp.int32)
    head = jnp.zeros((LANES, LANES), BF16).at[:classes].set(head_weight.T)
    masked, mask, rule, a, b = call(
        first_kernel,
        (BLOCK, WIDE_BLOCK, sds((32, LANES), F32), SIDE, SIDE),
        [SMEM, ANY, ANY, ANY],
        [pltpu.VMEM((VOX, LANES), BF16), pltpu.VMEM((1, VOX), jnp.int32), pltpu.SMEM((1, 27), jnp.int32), SEM((3,))],
    )(parity, features.reshape(VOX, LANES), occupancy.reshape(1, VOX), rulebook.reshape(1, 27))
    a, b = swap_a(a), swap_b(b)
    onehot, filter_here = call(labels_kernel, (WIDE_BLOCK, FILTER), [VMEM] * 2)(labels.reshape(1, VOX), filter_one)
    act_one, act_below, act_above, pre_one = call(
        one_kernel,
        (BLOCK, LAYER, LAYER, WIDE_BLOCK),
        [VMEM, SMEM] + [VMEM] * 5,
        [WIN_SCRATCH, pltpu.VMEM((128, 27 * LANES), BF16)],
        CONV,
    )(rule, parity, masked, a, b, filter_here, mask)
    win_two, grad_two, small, e, f = call(
        functools.partial(two_kernel, classes),
        (WINDOWS, BLOCK, sds((SMALL, LANES), F32), LAYER, LAYER),
        [VMEM, SMEM] + [VMEM] * 7,
        flops=CONV,
    )(rule, parity, act_one, act_below, act_above, filter_two, mask, onehot, head)
    e, f = swap_a(e), swap_b(f)
    terms_two, win_one = call(terms_kernel, (TERMS, WINDOWS), [VMEM, SMEM] + [VMEM] * 6, [WIDE_SCRATCH], CONV)(
        rule, parity, masked, a, b, win_two, grad_two, small
    )
    grad_one, terms_one, g, h = call(
        three_kernel,
        (BLOCK, TERMS, LAYER, LAYER),
        [VMEM, SMEM] + [VMEM] * 8,
        [WIN_SCRATCH, WIDE_SCRATCH],
        2 * CONV,
    )(rule, parity, grad_two, e, f, filter_two, mask, pre_one, win_one, small)
    g, h = swap_a(g), swap_b(h)
    grad_in, token = call(
        four_kernel, (BLOCK, sds((SMALL, LANES), F32)), [VMEM, SMEM] + [VMEM] * 5, [WIN_SCRATCH], CONV
    )(rule, parity, grad_one, g, h, filter_one, mask)
    peers = lax.axis_size("near") * lax.axis_size("x")
    rows = -(-27 * LANES // (peers * 16)) * 16
    away = jnp.where(core[0] == 0, terms_two, terms_one)
    chunks = call(
        functools.partial(pair_kernel, rows, peers),
        sds((peers, rows + 2 * SMALL, LANES), BF16),
        [SMEM] + [VMEM] * 3,
    )(core, terms_one, terms_two, core_swap(away))
    parts = lax.all_to_all(chunks, ("near", "x"), 0, 0, tiled=True)
    part = call(
        functools.partial(half_kernel, rows, peers), sds((rows + 2 * SMALL, LANES), BF16), [VMEM, ANY, ANY]
    )(parts, g, h)
    copies, head_sum, loss = call(
        functools.partial(copies_kernel, rows, peers, classes),
        (sds((peers, rows, LANES), BF16), sds((classes, LANES), F32), sds((1, LANES), F32)),
        [VMEM, VMEM, ANY],
    )(part, far_swap(part), token)
    whole = lax.all_to_all(copies, ("near", "x"), 0, 0, tiled=True)
    whole = whole.reshape(peers * rows, LANES)[: 27 * LANES].reshape(27, LANES, LANES)
    whole_other = core_swap(whole)
    scale = 1.0 / VOX
    return (
        jnp.where(core[0] == 0, whole, whole_other).astype(F32) * scale,
        jnp.where(core[0] == 0, whole_other, whole).astype(F32) * scale,
        head_sum.T,
        loss[0, 0],
        grad_in.reshape(features.shape),
    )


def solution(mesh):
    shape = mesh.devices.shape
    inner = Mesh(mesh.devices.reshape(2, shape[0] // 2, shape[1] // 2, 2), ("far", "near", "x", "core"))
    parts = ("x", "core")
    placed = (
        P(parts, SPACE, None, None),
        P(parts, SPACE, None),
        P(parts, SPACE, None),
        P(parts, SPACE, None),
        P(),
        P(),
        P(),
    )

    def whole(features, occupancy, labels, rulebook, filter_one, filter_two, head_weight):
        step = jax.shard_map(
            functools.partial(local, head_weight.shape[1]),
            mesh=inner,
            in_specs=placed,
            out_specs=(P(), P(), P(), P(), P(parts, SPACE, None, None)),
            check_vma=False,
        )
        return step(features, occupancy, labels, rulebook, filter_one, filter_two, head_weight)

    return whole
```

```python
import functools

import jax
import jax.numpy as jnp
from jax import lax
from jax.experimental import pallas as pl
from jax.experimental.pallas import tpu as pltpu
from jax.sharding import Mesh, PartitionSpec as P

EDGE = 8
VOX = 512
LANES = 128
TAPS = 9
SMALL = 8
SPACE = ("far", "near")
F32 = jnp.float32
BF16 = jnp.bfloat16
PARAMS = pltpu.CompilerParams(vmem_limit_bytes=16 * 1024 * 1024)
ROOMY = pltpu.CompilerParams(vmem_limit_bytes=62 * 1024 * 1024)
VMEM = pl.BlockSpec(memory_space=pltpu.VMEM)
ANY = pl.BlockSpec(memory_space=pl.ANY)
SMEM = pl.BlockSpec(memory_space=pltpu.SMEM)


def sds(shape, dtype):
    return jax.ShapeDtypeStruct(shape, dtype)


def contract(a, b, dim_a, dim_b):
    return lax.dot_general(a, b, (((dim_a,), (dim_b,)), ((), ())), preferred_element_type=F32)


def spread_layer(layer):
    return jnp.broadcast_to(layer.astype(F32).reshape(64, 1, LANES), (64, EDGE, LANES))


def from_sides(recv_a, recv_b):
    return recv_a.astype(F32), recv_b.astype(F32)


def build_windows(block, below, above, rule_ref, out_ref):
    cells = block.reshape(64, EDGE, LANES)
    depth = lax.broadcasted_iota(jnp.int32, (1, EDGE, LANES), 1)

    def flag(i, j, k, wanted):
        offset = 9 * i + 3 * j + k
        return jnp.where(rule_ref[offset : offset + 1, :] == wanted, 1.0, 0.0).reshape(1, 1, LANES)

    for k in range(3):
        if k == 1:
            own, other = cells, None
        elif k == 0:
            own, other = pltpu.roll(cells, 1, 1), spread_layer(below)
        else:
            own, other = pltpu.roll(cells, EDGE - 1, 1), spread_layer(above)
        own = own.reshape(EDGE, EDGE, EDGE, LANES)
        if other is not None:
            other = other.reshape(EDGE, EDGE, EDGE, LANES)

        def region(i, j):
            xs = {0: slice(7, 8), 1: slice(0, 8), 2: slice(0, 1)}[i]
            ys = {0: slice(7, 8), 1: slice(0, 8), 2: slice(0, 1)}[j]
            inner = flag(i, j, 1, 0)
            if k == 1:
                return own[xs, ys] * inner[None]
            edge = depth == (0 if k == 0 else EDGE - 1)
            keep = jnp.where(edge, flag(i, j, k, 0), inner)
            take = jnp.where(edge, flag(i, j, k, 1 if k == 0 else 2), 0.0)
            return own[xs, ys] * keep[None] + other[xs, ys] * take[None]

        columns = [jnp.concatenate([region(i, j) for i in range(3)], axis=0).astype(F32) for j in range(3)]
        for j in range(3):
            if j == 0:
                padded = jnp.concatenate([columns[0], columns[1][:, :7]], axis=1)
            elif j == 1:
                padded = columns[1]
            else:
                padded = jnp.concatenate([columns[1][:, 1:], columns[2]], axis=1)
            lane = (3 * j + k) * LANES
            out_ref[:, lane : lane + LANES] = padded.reshape(640, LANES).astype(BF16)


def put_sides(upward, downward, send_a_ref, send_b_ref):
    send_a_ref[...] = upward.astype(BF16)
    send_b_ref[...] = downward.astype(BF16)


def layers_of(block):
    cells = block.reshape(64, EDGE, LANES)
    return lambda z: cells[:, z, :]


def put_layers(block, send_a_ref, send_b_ref):
    layer = layers_of(block)
    put_sides(layer(EDGE - 1), layer(0), send_a_ref, send_b_ref)


def layer_windows(side, mine, touching, rule, out_ref, row):
    near, behind, wrap = (part.reshape(EDGE, EDGE, LANES) for part in side)
    mine = mine.reshape(EDGE, EDGE, LANES)
    across = 2 if touching == EDGE - 1 else 0
    width = lax.broadcasted_iota(jnp.int32, (1, EDGE, LANES), 1)

    def flag(i, j, k, wanted):
        offset = 9 * i + 3 * j + k
        return jnp.where(rule[offset : offset + 1, :] == wanted, 1.0, 0.0).reshape(1, 1, LANES)

    for k in range(3):
        sources = [(near if k == 1 else behind, 1, 0)]
        if k == across:
            sources = [(wrap, k, 0), (mine, k, 2 if across == 2 else 1)]
        for j in range(3):
            base = first = last = None
            for layer, region, wanted in sources:
                turned = layer if j == 1 else pltpu.roll(layer, 1 if j == 0 else EDGE - 1, 1)

                def gate(i):
                    inner = flag(i, 1, region, wanted)
                    if j == 1:
                        return inner
                    return jnp.where(width == (0 if j == 0 else EDGE - 1), flag(i, j, region, wanted), inner)

                parts = turned * gate(1), turned[7:8] * gate(0), turned[0:1] * gate(2)
                if base is None:
                    base, first, last = parts
                else:
                    base, first, last = base + parts[0], first + parts[1], last + parts[2]
            for i in range(3):
                cells = base
                if i == 0:
                    cells = jnp.concatenate([first, base[:7]], axis=0)
                elif i == 2:
                    cells = jnp.concatenate([base[1:], last], axis=0)
                lane = (9 * i + 3 * j + k) * LANES
                out_ref[row : row + 64, lane : lane + LANES] = cells.reshape(64, LANES).astype(BF16)


def forward_sum(win_ref, filt_ref):
    total = None
    for i in range(3):
        filt = filt_ref[TAPS * i : TAPS * (i + 1)].reshape(TAPS * LANES, LANES)
        term = jnp.dot(win_ref[64 * i : 64 * i + VOX, :], filt, preferred_element_type=F32)
        total = term if total is None else total + term
    return total


def backward_sum(win_ref, filt_ref):
    total = None
    for i in range(3):
        filt = jnp.concatenate([filt_ref[26 - TAPS * i - t] for t in range(TAPS)], axis=1)
        term = contract(win_ref[64 * i : 64 * i + VOX, :], filt, 1, 1)
        total = term if total is None else total + term
    return total


def filter_terms(win_ref, grad, small_ref, wide_ref, out_ref):
    pair = split_pair(small_ref[: SMALL // 2])
    out_ref[27] = jnp.concatenate([pair, jnp.zeros((LANES - SMALL, LANES), F32)], axis=0).astype(BF16)
    wide_ref[...] = jnp.zeros_like(wide_ref)
    for i in range(3):
        wide_ref[64 * i : 64 * i + VOX, LANES * i : LANES * (i + 1)] = grad
    for t in range(TAPS):
        term = contract(win_ref[:, LANES * t : LANES * (t + 1)], wide_ref[...], 0, 0)
        for i in range(3):
            out_ref[TAPS * i + t] = term[:, LANES * i : LANES * (i + 1)].astype(BF16)


def silu_parts(pre):
    sigmoid = 1.0 / (1.0 + jnp.exp(-pre))
    return pre * sigmoid, sigmoid * (1.0 + pre * (1.0 - sigmoid))


def filled_rows(occ):
    rows = lax.broadcasted_iota(jnp.int32, (SMALL, VOX), 0)
    occ_rows = jnp.where(rows == 0, jnp.broadcast_to(occ, (SMALL, VOX)), 0).astype(F32).astype(BF16)
    row = lax.broadcasted_iota(jnp.int32, (SMALL, LANES), 0)
    return contract(occ_rows, jnp.where(row == 0, 1.0, 0.0).astype(BF16), 0, 0)


def first_kernel(feat_hbm, occ_hbm, rule_hbm, send_a, send_b, feat, occ, rule, sems):
    copies = [
        pltpu.make_async_copy(feat_hbm, feat, sems.at[0]),
        pltpu.make_async_copy(occ_hbm, occ, sems.at[1]),
        pltpu.make_async_copy(rule_hbm, rule, sems.at[2]),
    ]
    for copy in copies:
        copy.start()
    for copy in copies:
        copy.wait()
    filled = filled_rows(occ[...])
    block = feat[...].astype(F32) * filled
    offsets = lax.broadcasted_iota(jnp.int32, (32, LANES), 0)
    found = jnp.zeros((32, LANES), jnp.int32)
    for o in range(27):
        found = jnp.where(offsets == o, rule[0, o], found)
    found = found.astype(F32)
    layer, held = layers_of(block), layers_of(filled)
    top = EDGE - 1
    upward = jnp.concatenate([layer(top), layer(top - 1), layer(0), held(top), found], axis=0)
    downward = jnp.concatenate([layer(0), layer(1), layer(top), held(0), found], axis=0)
    put_sides(upward, downward, send_a, send_b)


def prep_kernel(feat, occ, found, filt_in, masked, mask, rule, filt):
    filt[...] = filt_in[...]
    row = lax.broadcasted_iota(jnp.int32, (SMALL, 27), 0)
    rule_rows = jnp.where(row == 0, jnp.broadcast_to(found[...], (SMALL, 27)), 0).astype(F32).astype(BF16)
    one_row = lax.broadcasted_iota(jnp.int32, (SMALL, LANES), 0)
    rule[...] = contract(rule_rows, jnp.where(one_row == 0, 1.0, 0.0).astype(BF16), 0, 0)
    filled = filled_rows(occ[...])
    mask[...] = filled
    masked[...] = (feat[...].astype(F32) * filled).astype(BF16)


def one_kernel(rule, masked, mask, recv_a, recv_b, filt, act, act_below, act_above, pre, win, rim):
    below, above = from_sides(recv_a[...], recv_b[...])
    block = masked[...].astype(F32)
    build_windows(block, below[:64], above[:64], rule, win)
    total = forward_sum(win, filt) * mask[...]
    pre[...] = total
    acted, _ = silu_parts(total)
    act[...] = acted.astype(BF16)
    layer = layers_of(block)
    for side, mine, touching, row in ((below, layer(0), EDGE - 1, 0), (above, layer(EDGE - 1), 0, 64)):
        parts = [side[at : at + 64] for at in (0, 64, 128)]
        layer_windows(parts, mine, touching, side[256:288], rim, row)
    total = None
    wide = TAPS * LANES
    for i in range(3):
        weights = filt[TAPS * i : TAPS * (i + 1)].reshape(wide, LANES)
        term = jnp.dot(rim[:, wide * i : wide * (i + 1)], weights, preferred_element_type=F32)
        total = term if total is None else total + term
    for side, row, out in ((below, 0, act_below), (above, 64, act_above)):
        acted, _ = silu_parts(total[row : row + 64] * side[192:256])
        out[...] = acted.astype(BF16)


def two_kernel(
    classes, rule, act_one, act_below, act_above, filt, mask, labels, head_rows,
    win, grad, small, send_a, send_b,
):
    build_windows(act_one[...].astype(F32), act_below[...].astype(F32), act_above[...].astype(F32), rule, win)
    head = jnp.concatenate([head_rows[...].astype(F32), jnp.zeros((LANES - classes, LANES), F32)], axis=0).astype(BF16)
    rows = lax.broadcasted_iota(jnp.int32, (SMALL, VOX), 0)
    hot_rows = jnp.where(rows == jnp.broadcast_to(labels[...], (SMALL, VOX)), 1.0, 0.0).astype(BF16)
    unit_row = lax.broadcasted_iota(jnp.int32, (SMALL, LANES), 0)
    unit_lane = lax.broadcasted_iota(jnp.int32, (SMALL, LANES), 1)
    hot = contract(hot_rows, jnp.where(unit_row == unit_lane, 1.0, 0.0).astype(BF16), 0, 0)
    filled = mask[...]
    pre = forward_sum(win, filt) * filled
    acted, slope = silu_parts(pre)
    acted = acted.astype(BF16)
    lane = lax.broadcasted_iota(jnp.int32, (VOX, LANES), 1)
    logits = contract(acted, head, 1, 1)
    known = lane < classes
    top = jnp.max(jnp.where(known, logits, -jnp.inf), axis=1, keepdims=True)
    powers = jnp.where(known, jnp.exp(jnp.where(known, logits - top, 0.0)), 0.0)
    total_log = top + jnp.log(jnp.sum(powers, axis=1, keepdims=True))
    chances = jnp.where(known, jnp.exp(jnp.where(known, logits - total_log, 0.0)), 0.0)
    dlogits = (chances - hot) * filled
    high = dlogits.astype(BF16)
    low = (dlogits - high.astype(F32)).astype(BF16)
    back = jnp.dot(high, head, preferred_element_type=F32) + jnp.dot(low, head, preferred_element_type=F32)
    out = (back * slope * filled).astype(BF16)
    grad[...] = out
    put_layers(out.astype(F32), send_a, send_b)
    head_terms = (contract(high, acted, 0, 0) + contract(low, acted, 0, 0))[:SMALL]
    losses = jnp.sum((total_log - logits) * hot * filled, axis=0, keepdims=True)
    counted = jnp.sum(filled, axis=0, keepdims=True)
    tail = jnp.where(lane[:1] < classes, losses, jnp.where(lane[:1] == classes, counted, 0.0))
    row = lax.broadcasted_iota(jnp.int32, (SMALL, LANES), 0)
    values = jnp.where(row < classes, head_terms, jnp.where(row == classes, tail, 0.0))
    small[...] = values


def terms_kernel(rule, masked, recv_a, recv_b, win_two, grad, small, out, win_one, wide):
    filter_terms(win_two, grad[...], small, wide, out)
    below, above = from_sides(recv_a[...], recv_b[...])
    build_windows(masked[...].astype(F32), below[:64], above[:64], rule, win_one)


def three_kernel(
    rule, grad_two, recv_a, recv_b, filt, mask, pre, win_one, small,
    grad_one, terms, send_a, send_b, win, wide,
):
    below, above = from_sides(recv_a[...], recv_b[...])
    build_windows(grad_two[...].astype(F32), below, above, rule, win)
    _, slope = silu_parts(pre[...])
    out = (backward_sum(win, filt) * slope * mask[...]).astype(BF16)
    grad_one[...] = out
    put_layers(out.astype(F32), send_a, send_b)
    filter_terms(win_one, out, small, wide, terms)


def four_kernel(rule, grad_one, recv_a, recv_b, filt, mask, later, out, win):
    below, above = from_sides(recv_a[...], recv_b[...])
    build_windows(grad_one[...].astype(F32), below, above, rule, win)
    total = backward_sum(win, filt) * mask[...]
    out[...] = total.astype(BF16)


def call(kernel, outs, specs, scratch=(), flops=0, params=PARAMS):
    return pl.pallas_call(
        kernel,
        out_shape=outs,
        in_specs=specs,
        out_specs=jax.tree.map(lambda _: VMEM, outs),
        scratch_shapes=list(scratch),
        compiler_params=params,
        cost_estimate=pl.CostEstimate(flops=flops, bytes_accessed=4_000_000, transcendentals=0),
    )


BLOCK = sds((VOX, LANES), BF16)
WIDE_BLOCK = sds((VOX, LANES), F32)
LAYER = sds((64, LANES), BF16)
FILTER = sds((27, LANES, LANES), BF16)
SIDE = sds((288, LANES), BF16)
WINDOWS = sds((640, TAPS * LANES), BF16)
TERMS = sds((28, LANES, LANES), BF16)
WIN_SCRATCH = pltpu.VMEM((640, TAPS * LANES), BF16)
SEM = pltpu.SemaphoreType.DMA
WIDE_SCRATCH = pltpu.VMEM((640, 3 * LANES), BF16)
CONV = 2 * 27 * VOX * LANES * LANES


def send_up(value):
    length = lax.axis_size(SPACE)
    return lax.ppermute(value, SPACE, [(i, (i + 1) % length) for i in range(length)])


def send_down(value):
    length = lax.axis_size(SPACE)
    return lax.ppermute(value, SPACE, [(i, (i - 1) % length) for i in range(length)])


def far_swap(value):
    return lax.ppermute(value, "far", [(0, 1), (1, 0)])


def core_swap(value):
    return lax.ppermute(value, "core", [(0, 1), (1, 0)])


def split_pair(value):
    high = value.astype(BF16).astype(F32)
    return jnp.concatenate([high, value - high], axis=0)


def join_pair(pair):
    return pair[: SMALL // 2] + pair[SMALL // 2 : SMALL]


def pair_kernel(rows, peers, core, one, two, other, out):
    small = join_pair(one[27].astype(F32)) + join_pair(other[27].astype(F32))
    tail = jnp.concatenate([split_pair(small), jnp.zeros((SMALL, LANES), F32)], axis=0)
    mine = jnp.where(core[0] == 0, one[:27], two[:27])
    total = mine.reshape(27 * LANES, LANES).astype(F32) + other[:27].reshape(27 * LANES, LANES).astype(F32)
    spare = rows * peers - 27 * LANES
    if spare:
        total = jnp.concatenate([total, jnp.zeros((spare, LANES), F32)], axis=0)
    for p in range(peers):
        out[p] = jnp.concatenate([total[p * rows : (p + 1) * rows], tail], axis=0).astype(BF16)


def half_kernel(rows, peers, parts, out):
    total = parts[0].astype(F32)
    for p in range(1, peers):
        total = total + parts[p].astype(F32)
    tail = split_pair(join_pair(total[rows : rows + SMALL]))
    out[...] = jnp.concatenate([total[:rows], tail, jnp.zeros((SMALL, LANES), F32)], axis=0).astype(BF16)


def copies_kernel(rows, peers, classes, mine, other, later_a, later_b, out, head, loss):
    a, b = mine[...].astype(F32), other[...].astype(F32)
    both = (a[:rows] + b[:rows]).astype(BF16)
    for p in range(peers):
        out[p] = both
    tail = join_pair(a[rows:]) + join_pair(b[rows:])
    head[...] = tail[:classes] * (1.0 / VOX)
    last = tail[classes : classes + 1]
    lane = lax.broadcasted_iota(jnp.int32, (1, LANES), 1)
    losses = jnp.sum(jnp.where(lane < classes, last, 0.0), axis=1, keepdims=True)
    counted = jnp.sum(jnp.where(lane == classes, last, 0.0), axis=1, keepdims=True)
    loss[...] = jnp.broadcast_to(losses / counted, (1, LANES))


def local(classes, features, occupancy, labels, rulebook, filter_one, filter_two, head_weight):
    core = lax.axis_index("core").reshape(1).astype(jnp.int32)
    inputs = features.reshape(VOX, LANES), occupancy.reshape(1, VOX), rulebook.reshape(1, 27)
    a, b = call(
        first_kernel,
        (SIDE, SIDE),
        [ANY] * 3,
        [pltpu.VMEM((VOX, LANES), BF16), pltpu.VMEM((1, VOX), jnp.int32), pltpu.SMEM((1, 27), jnp.int32), SEM((3,))],
        params=ROOMY,
    )(*inputs)
    a, b = send_up(a), send_down(b)
    masked, mask, rule, filter_here = call(
        prep_kernel, (BLOCK, WIDE_BLOCK, sds((27, LANES), F32), FILTER), [VMEM] * 4
    )(*inputs, filter_one)
    act_one, act_below, act_above, pre_one = call(
        one_kernel,
        (BLOCK, LAYER, LAYER, WIDE_BLOCK),
        [VMEM] * 6,
        [WIN_SCRATCH, pltpu.VMEM((128, 27 * LANES), BF16)],
        CONV,
    )(rule, masked, mask, a, b, filter_here)
    win_two, grad_two, small, e, f = call(
        functools.partial(two_kernel, classes),
        (WINDOWS, BLOCK, sds((SMALL, LANES), F32), LAYER, LAYER),
        [VMEM] + [VMEM] * 7,
        flops=CONV,
    )(rule, act_one, act_below, act_above, filter_two, mask, labels.reshape(1, VOX), head_weight.T)
    e, f = send_up(e), send_down(f)
    terms_two, win_one = call(terms_kernel, (TERMS, WINDOWS), [VMEM] + [VMEM] * 6, [WIDE_SCRATCH], CONV)(
        rule, masked, a, b, win_two, grad_two, small
    )
    grad_one, terms_one, g, h = call(
        three_kernel,
        (BLOCK, TERMS, LAYER, LAYER),
        [VMEM] + [VMEM] * 8,
        [WIN_SCRATCH, WIDE_SCRATCH],
        2 * CONV,
    )(rule, grad_two, e, f, filter_two, mask, pre_one, win_one, small)
    g, h = send_up(g), send_down(h)
    peers = lax.axis_size("near") * lax.axis_size("x")
    rows = -(-27 * LANES // (peers * 16)) * 16
    away = jnp.where(core[0] == 0, terms_two, terms_one)
    chunks = call(
        functools.partial(pair_kernel, rows, peers),
        sds((peers, rows + 2 * SMALL, LANES), BF16),
        [SMEM] + [VMEM] * 3,
    )(core, terms_one, terms_two, core_swap(away))
    parts = lax.all_to_all(chunks, ("near", "x"), 0, 0, tiled=True)
    part = call(
        functools.partial(half_kernel, rows, peers), sds((rows + 2 * SMALL, LANES), BF16), [VMEM]
    )(parts)
    copies, head_sum, loss = call(
        functools.partial(copies_kernel, rows, peers, classes),
        (sds((peers, rows, LANES), BF16), sds((classes, LANES), F32), sds((1, LANES), F32)),
        [VMEM, VMEM, ANY, ANY],
    )(part, far_swap(part), g, h)
    whole = lax.all_to_all(copies, ("near", "x"), 0, 0, tiled=True)
    whole = whole.reshape(peers * rows, LANES)[: 27 * LANES].reshape(27, LANES, LANES)
    whole_other = core_swap(whole)
    grad_in = call(four_kernel, BLOCK, [VMEM] + [VMEM] * 5 + [ANY], [WIN_SCRATCH], CONV)(
        rule, grad_one, g, h, filter_one, mask, whole
    )
    scale = 1.0 / VOX
    return (
        jnp.where(core[0] == 0, whole, whole_other).astype(F32) * scale,
        jnp.where(core[0] == 0, whole_other, whole).astype(F32) * scale,
        head_sum.T,
        loss[0, 0],
        grad_in.reshape(features.shape),
    )


def solution(mesh):
    shape = mesh.devices.shape
    inner = Mesh(mesh.devices.reshape(2, shape[0] // 2, shape[1] // 2, 2), ("far", "near", "x", "core"))
    parts = ("x", "core")
    placed = (
        P(parts, SPACE, None, None),
        P(parts, SPACE, None),
        P(parts, SPACE, None),
        P(parts, SPACE, None),
        P(),
        P(),
        P(),
    )

    def whole(features, occupancy, labels, rulebook, filter_one, filter_two, head_weight):
        step = jax.shard_map(
            functools.partial(local, head_weight.shape[1]),
            mesh=inner,
            in_specs=placed,
            out_specs=(P(), P(), P(), P(), P(parts, SPACE, None, None)),
            check_vma=False,
        )
        return step(features, occupancy, labels, rulebook, filter_one, filter_two, head_weight)

    return whole
```

```python
import functools

import jax
import jax.numpy as jnp
from jax import lax
from jax.experimental import pallas as pl
from jax.experimental.pallas import tpu as pltpu
from jax.sharding import Mesh, PartitionSpec as P

EDGE = 8
VOX = 512
LANES = 128
TAPS = 9
SMALL = 8
SPACE = ("far", "near")
F32 = jnp.float32
BF16 = jnp.bfloat16
PARAMS = pltpu.CompilerParams(vmem_limit_bytes=16 * 1024 * 1024)
ROOMY = pltpu.CompilerParams(vmem_limit_bytes=62 * 1024 * 1024)
VMEM = pl.BlockSpec(memory_space=pltpu.VMEM)
ANY = pl.BlockSpec(memory_space=pl.ANY)
SMEM = pl.BlockSpec(memory_space=pltpu.SMEM)


def sds(shape, dtype):
    return jax.ShapeDtypeStruct(shape, dtype)


def contract(a, b, dim_a, dim_b):
    return lax.dot_general(a, b, (((dim_a,), (dim_b,)), ((), ())), preferred_element_type=F32)


def spread_layer(layer):
    return jnp.broadcast_to(layer.astype(F32).reshape(64, 1, LANES), (64, EDGE, LANES))


def from_sides(parity_ref, recv_a, recv_b):
    even = parity_ref[0] == 0
    got_a, got_b = recv_a.astype(F32), recv_b.astype(F32)
    return jnp.where(even, got_b, got_a), jnp.where(even, got_a, got_b)


def build_windows(block, below, above, rule_ref, out_ref):
    cells = block.reshape(64, EDGE, LANES)
    depth = lax.broadcasted_iota(jnp.int32, (1, EDGE, LANES), 1)

    def flag(i, j, k, wanted):
        offset = 9 * i + 3 * j + k
        return jnp.where(rule_ref[offset : offset + 1, :] == wanted, 1.0, 0.0).reshape(1, 1, LANES)

    for k in range(3):
        if k == 1:
            own, other = cells, None
        elif k == 0:
            own, other = pltpu.roll(cells, 1, 1), spread_layer(below)
        else:
            own, other = pltpu.roll(cells, EDGE - 1, 1), spread_layer(above)
        own = own.reshape(EDGE, EDGE, EDGE, LANES)
        if other is not None:
            other = other.reshape(EDGE, EDGE, EDGE, LANES)

        def region(i, j):
            xs = {0: slice(7, 8), 1: slice(0, 8), 2: slice(0, 1)}[i]
            ys = {0: slice(7, 8), 1: slice(0, 8), 2: slice(0, 1)}[j]
            inner = flag(i, j, 1, 0)
            if k == 1:
                return own[xs, ys] * inner[None]
            edge = depth == (0 if k == 0 else EDGE - 1)
            keep = jnp.where(edge, flag(i, j, k, 0), inner)
            take = jnp.where(edge, flag(i, j, k, 1 if k == 0 else 2), 0.0)
            return own[xs, ys] * keep[None] + other[xs, ys] * take[None]

        columns = [jnp.concatenate([region(i, j) for i in range(3)], axis=0).astype(F32) for j in range(3)]
        for j in range(3):
            if j == 0:
                padded = jnp.concatenate([columns[0], columns[1][:, :7]], axis=1)
            elif j == 1:
                padded = columns[1]
            else:
                padded = jnp.concatenate([columns[1][:, 1:], columns[2]], axis=1)
            lane = (3 * j + k) * LANES
            out_ref[:, lane : lane + LANES] = padded.reshape(640, LANES).astype(BF16)


def put_sides(parity_ref, upward, downward, send_a_ref, send_b_ref):
    even = parity_ref[0] == 0
    send_a_ref[...] = jnp.where(even, upward, downward).astype(BF16)
    send_b_ref[...] = jnp.where(even, downward, upward).astype(BF16)


def layers_of(block):
    cells = block.reshape(64, EDGE, LANES)
    return lambda z: cells[:, z, :]


def put_layers(block, parity_ref, send_a_ref, send_b_ref):
    layer = layers_of(block)
    put_sides(parity_ref, layer(EDGE - 1), layer(0), send_a_ref, send_b_ref)


def layer_windows(side, mine, touching, rule, out_ref, row):
    near, behind, wrap = (part.reshape(EDGE, EDGE, LANES) for part in side)
    mine = mine.reshape(EDGE, EDGE, LANES)
    across = 2 if touching == EDGE - 1 else 0
    width = lax.broadcasted_iota(jnp.int32, (1, EDGE, LANES), 1)

    def flag(i, j, k, wanted):
        offset = 9 * i + 3 * j + k
        return jnp.where(rule[offset : offset + 1, :] == wanted, 1.0, 0.0).reshape(1, 1, LANES)

    for k in range(3):
        sources = [(near if k == 1 else behind, 1, 0)]
        if k == across:
            sources = [(wrap, k, 0), (mine, k, 2 if across == 2 else 1)]
        for j in range(3):
            base = first = last = None
            for layer, region, wanted in sources:
                turned = layer if j == 1 else pltpu.roll(layer, 1 if j == 0 else EDGE - 1, 1)

                def gate(i):
                    inner = flag(i, 1, region, wanted)
                    if j == 1:
                        return inner
                    return jnp.where(width == (0 if j == 0 else EDGE - 1), flag(i, j, region, wanted), inner)

                parts = turned * gate(1), turned[7:8] * gate(0), turned[0:1] * gate(2)
                if base is None:
                    base, first, last = parts
                else:
                    base, first, last = base + parts[0], first + parts[1], last + parts[2]
            for i in range(3):
                cells = base
                if i == 0:
                    cells = jnp.concatenate([first, base[:7]], axis=0)
                elif i == 2:
                    cells = jnp.concatenate([base[1:], last], axis=0)
                lane = (9 * i + 3 * j + k) * LANES
                out_ref[row : row + 64, lane : lane + LANES] = cells.reshape(64, LANES).astype(BF16)


def forward_sum(win_ref, filt_ref):
    total = None
    for i in range(3):
        filt = filt_ref[TAPS * i : TAPS * (i + 1)].reshape(TAPS * LANES, LANES)
        term = jnp.dot(win_ref[64 * i : 64 * i + VOX, :], filt, preferred_element_type=F32)
        total = term if total is None else total + term
    return total


def backward_sum(win_ref, filt_ref):
    total = None
    for i in range(3):
        filt = jnp.concatenate([filt_ref[26 - TAPS * i - t] for t in range(TAPS)], axis=1)
        term = contract(win_ref[64 * i : 64 * i + VOX, :], filt, 1, 1)
        total = term if total is None else total + term
    return total


def filter_terms(win_ref, grad, small_ref, wide_ref, out_ref):
    pair = split_pair(small_ref[: SMALL // 2])
    out_ref[27] = jnp.concatenate([pair, jnp.zeros((LANES - SMALL, LANES), F32)], axis=0).astype(BF16)
    wide_ref[...] = jnp.zeros_like(wide_ref)
    for i in range(3):
        wide_ref[64 * i : 64 * i + VOX, LANES * i : LANES * (i + 1)] = grad
    for t in range(TAPS):
        term = contract(win_ref[:, LANES * t : LANES * (t + 1)], wide_ref[...], 0, 0)
        for i in range(3):
            out_ref[TAPS * i + t] = term[:, LANES * i : LANES * (i + 1)].astype(BF16)


def silu_parts(pre):
    sigmoid = 1.0 / (1.0 + jnp.exp(-pre))
    return pre * sigmoid, sigmoid * (1.0 + pre * (1.0 - sigmoid))


def filled_rows(occ):
    rows = lax.broadcasted_iota(jnp.int32, (SMALL, VOX), 0)
    occ_rows = jnp.where(rows == 0, jnp.broadcast_to(occ, (SMALL, VOX)), 0).astype(F32).astype(BF16)
    row = lax.broadcasted_iota(jnp.int32, (SMALL, LANES), 0)
    return contract(occ_rows, jnp.where(row == 0, 1.0, 0.0).astype(BF16), 0, 0)


def first_kernel(parity, feat_hbm, occ_hbm, rule_hbm, send_a, send_b, feat, occ, rule, sems):
    copies = [
        pltpu.make_async_copy(feat_hbm, feat, sems.at[0]),
        pltpu.make_async_copy(occ_hbm, occ, sems.at[1]),
        pltpu.make_async_copy(rule_hbm, rule, sems.at[2]),
    ]
    for copy in copies:
        copy.start()
    for copy in copies:
        copy.wait()
    filled = filled_rows(occ[...])
    block = feat[...].astype(F32) * filled
    offsets = lax.broadcasted_iota(jnp.int32, (32, LANES), 0)
    found = jnp.zeros((32, LANES), jnp.int32)
    for o in range(27):
        found = jnp.where(offsets == o, rule[0, o], found)
    found = found.astype(F32)
    layer, held = layers_of(block), layers_of(filled)
    top = EDGE - 1
    upward = jnp.concatenate([layer(top), layer(top - 1), layer(0), held(top), found], axis=0)
    downward = jnp.concatenate([layer(0), layer(1), layer(top), held(0), found], axis=0)
    put_sides(parity, upward, downward, send_a, send_b)


def prep_kernel(feat, occ, found, filt_in, masked, mask, rule, filt):
    filt[...] = filt_in[...]
    row = lax.broadcasted_iota(jnp.int32, (SMALL, 27), 0)
    rule_rows = jnp.where(row == 0, jnp.broadcast_to(found[...], (SMALL, 27)), 0).astype(F32).astype(BF16)
    one_row = lax.broadcasted_iota(jnp.int32, (SMALL, LANES), 0)
    rule[...] = contract(rule_rows, jnp.where(one_row == 0, 1.0, 0.0).astype(BF16), 0, 0)
    filled = filled_rows(occ[...])
    mask[...] = filled
    masked[...] = (feat[...].astype(F32) * filled).astype(BF16)


def one_kernel(parity, rule, masked, mask, recv_a, recv_b, filt, act, act_below, act_above, pre, win, rim):
    below, above = from_sides(parity, recv_a[...], recv_b[...])
    block = masked[...].astype(F32)
    build_windows(block, below[:64], above[:64], rule, win)
    total = forward_sum(win, filt) * mask[...]
    pre[...] = total
    acted, _ = silu_parts(total)
    act[...] = acted.astype(BF16)
    layer = layers_of(block)
    for side, mine, touching, row in ((below, layer(0), EDGE - 1, 0), (above, layer(EDGE - 1), 0, 64)):
        parts = [side[at : at + 64] for at in (0, 64, 128)]
        layer_windows(parts, mine, touching, side[256:288], rim, row)
    total = None
    wide = TAPS * LANES
    for i in range(3):
        weights = filt[TAPS * i : TAPS * (i + 1)].reshape(wide, LANES)
        term = jnp.dot(rim[:, wide * i : wide * (i + 1)], weights, preferred_element_type=F32)
        total = term if total is None else total + term
    for side, row, out in ((below, 0, act_below), (above, 64, act_above)):
        acted, _ = silu_parts(total[row : row + 64] * side[192:256])
        out[...] = acted.astype(BF16)


def two_kernel(
    classes, parity, rule, act_one, act_below, act_above, filt, mask, labels, head_rows,
    win, grad, small, send_a, send_b,
):
    build_windows(act_one[...].astype(F32), act_below[...].astype(F32), act_above[...].astype(F32), rule, win)
    head = jnp.concatenate([head_rows[...].astype(F32), jnp.zeros((LANES - classes, LANES), F32)], axis=0).astype(BF16)
    rows = lax.broadcasted_iota(jnp.int32, (SMALL, VOX), 0)
    hot_rows = jnp.where(rows == jnp.broadcast_to(labels[...], (SMALL, VOX)), 1.0, 0.0).astype(BF16)
    unit_row = lax.broadcasted_iota(jnp.int32, (SMALL, LANES), 0)
    unit_lane = lax.broadcasted_iota(jnp.int32, (SMALL, LANES), 1)
    hot = contract(hot_rows, jnp.where(unit_row == unit_lane, 1.0, 0.0).astype(BF16), 0, 0)
    filled = mask[...]
    pre = forward_sum(win, filt) * filled
    acted, slope = silu_parts(pre)
    acted = acted.astype(BF16)
    lane = lax.broadcasted_iota(jnp.int32, (VOX, LANES), 1)
    logits = contract(acted, head, 1, 1)
    known = lane < classes
    top = jnp.max(jnp.where(known, logits, -jnp.inf), axis=1, keepdims=True)
    powers = jnp.where(known, jnp.exp(jnp.where(known, logits - top, 0.0)), 0.0)
    total_log = top + jnp.log(jnp.sum(powers, axis=1, keepdims=True))
    chances = jnp.where(known, jnp.exp(jnp.where(known, logits - total_log, 0.0)), 0.0)
    dlogits = (chances - hot) * filled
    high = dlogits.astype(BF16)
    low = (dlogits - high.astype(F32)).astype(BF16)
    back = jnp.dot(high, head, preferred_element_type=F32) + jnp.dot(low, head, preferred_element_type=F32)
    out = (back * slope * filled).astype(BF16)
    grad[...] = out
    put_layers(out.astype(F32), parity, send_a, send_b)
    head_terms = (contract(high, acted, 0, 0) + contract(low, acted, 0, 0))[:SMALL]
    losses = jnp.sum((total_log - logits) * hot * filled, axis=0, keepdims=True)
    counted = jnp.sum(filled, axis=0, keepdims=True)
    tail = jnp.where(lane[:1] < classes, losses, jnp.where(lane[:1] == classes, counted, 0.0))
    row = lax.broadcasted_iota(jnp.int32, (SMALL, LANES), 0)
    values = jnp.where(row < classes, head_terms, jnp.where(row == classes, tail, 0.0))
    small[...] = values


def terms_kernel(parity, rule, masked, recv_a, recv_b, win_two, grad, small, out, win_one, wide):
    filter_terms(win_two, grad[...], small, wide, out)
    below, above = from_sides(parity, recv_a[...], recv_b[...])
    build_windows(masked[...].astype(F32), below[:64], above[:64], rule, win_one)


def three_kernel(
    parity, rule, grad_two, recv_a, recv_b, filt, mask, pre, win_one, small,
    grad_one, terms, send_a, send_b, win, wide,
):
    below, above = from_sides(parity, recv_a[...], recv_b[...])
    build_windows(grad_two[...].astype(F32), below, above, rule, win)
    _, slope = silu_parts(pre[...])
    out = (backward_sum(win, filt) * slope * mask[...]).astype(BF16)
    grad_one[...] = out
    put_layers(out.astype(F32), parity, send_a, send_b)
    filter_terms(win_one, out, small, wide, terms)


def four_kernel(parity, rule, grad_one, recv_a, recv_b, filt, mask, out, win):
    below, above = from_sides(parity, recv_a[...], recv_b[...])
    build_windows(grad_one[...].astype(F32), below, above, rule, win)
    total = backward_sum(win, filt) * mask[...]
    out[...] = total.astype(BF16)


def own_kernel(core, whole, one, two, wide, sems):
    for part in range(3):
        at = pl.ds(TAPS * part, TAPS)
        wide[at] = whole[at].astype(F32) * (1.0 / VOX)
        for wanted, out in ((0, one), (1, two)):
            pl.when(core[0] == wanted)(pltpu.make_async_copy(wide.at[at], out.at[at], sems.at[part]).start)
    for part in range(3):
        at = pl.ds(TAPS * part, TAPS)
        pltpu.make_async_copy(wide.at[at], one.at[at], sems.at[part]).wait()


def other_kernel(core, whole, one_in, two_in, one, two, wide, sems):
    own_kernel(core, whole, one, two, wide, sems)


def call(kernel, outs, specs, scratch=(), flops=0, params=PARAMS, out_specs=None, alias=None):
    return pl.pallas_call(
        kernel,
        out_shape=outs,
        in_specs=specs,
        out_specs=jax.tree.map(lambda _: VMEM, outs) if out_specs is None else out_specs,
        input_output_aliases=alias or {},
        scratch_shapes=list(scratch),
        compiler_params=params,
        cost_estimate=pl.CostEstimate(flops=flops, bytes_accessed=4_000_000, transcendentals=0),
    )


BLOCK = sds((VOX, LANES), BF16)
WIDE_BLOCK = sds((VOX, LANES), F32)
LAYER = sds((64, LANES), BF16)
FILTER = sds((27, LANES, LANES), BF16)
SIDE = sds((288, LANES), BF16)
WINDOWS = sds((640, TAPS * LANES), BF16)
TERMS = sds((28, LANES, LANES), BF16)
WIN_SCRATCH = pltpu.VMEM((640, TAPS * LANES), BF16)
SEM = pltpu.SemaphoreType.DMA
WIDE_SCRATCH = pltpu.VMEM((640, 3 * LANES), BF16)
CONV = 2 * 27 * VOX * LANES * LANES


def swap_a(value):
    length = lax.axis_size(SPACE)
    return lax.ppermute(value, SPACE, [(i, i ^ 1) for i in range(length)])


def swap_b(value):
    length = lax.axis_size(SPACE)
    pairs = []
    for i in range(length):
        to = i + 1 if i % 2 else i - 1
        for c in range(2):
            pairs.append((2 * i + c, 2 * to + c if 0 <= to < length else 2 * i + 1 - c))
    return lax.ppermute(value, SPACE + ("core",), pairs)


def far_swap(value):
    return lax.ppermute(value, "far", [(0, 1), (1, 0)])


def core_swap(value):
    return lax.ppermute(value, "core", [(0, 1), (1, 0)])


def split_pair(value):
    high = value.astype(BF16).astype(F32)
    return jnp.concatenate([high, value - high], axis=0)


def join_pair(pair):
    return pair[: SMALL // 2] + pair[SMALL // 2 : SMALL]


def pair_kernel(rows, peers, core, one, two, other, out):
    small = join_pair(one[27].astype(F32)) + join_pair(other[27].astype(F32))
    tail = jnp.concatenate([split_pair(small), jnp.zeros((SMALL, LANES), F32)], axis=0)
    mine = jnp.where(core[0] == 0, one[:27], two[:27])
    total = mine.reshape(27 * LANES, LANES).astype(F32) + other[:27].reshape(27 * LANES, LANES).astype(F32)
    spare = rows * peers - 27 * LANES
    if spare:
        total = jnp.concatenate([total, jnp.zeros((spare, LANES), F32)], axis=0)
    for p in range(peers):
        out[p] = jnp.concatenate([total[p * rows : (p + 1) * rows], tail], axis=0).astype(BF16)


def half_kernel(rows, peers, parts, out):
    total = parts[0].astype(F32)
    for p in range(1, peers):
        total = total + parts[p].astype(F32)
    tail = split_pair(join_pair(total[rows : rows + SMALL]))
    out[...] = jnp.concatenate([total[:rows], tail, jnp.zeros((SMALL, LANES), F32)], axis=0).astype(BF16)


def copies_kernel(rows, peers, classes, mine, other, later_a, later_b, out, head, loss):
    a, b = mine[...].astype(F32), other[...].astype(F32)
    both = (a[:rows] + b[:rows]).astype(BF16)
    for p in range(peers):
        out[p] = both
    tail = join_pair(a[rows:]) + join_pair(b[rows:])
    head[...] = tail[:classes] * (1.0 / VOX)
    last = tail[classes : classes + 1]
    lane = lax.broadcasted_iota(jnp.int32, (1, LANES), 1)
    losses = jnp.sum(jnp.where(lane < classes, last, 0.0), axis=1, keepdims=True)
    counted = jnp.sum(jnp.where(lane == classes, last, 0.0), axis=1, keepdims=True)
    loss[...] = jnp.broadcast_to(losses / counted, (1, LANES))


def local(classes, features, occupancy, labels, rulebook, filter_one, filter_two, head_weight):
    parity = (lax.axis_index(SPACE) % 2).reshape(1).astype(jnp.int32)
    core = lax.axis_index("core").reshape(1).astype(jnp.int32)
    inputs = features.reshape(VOX, LANES), occupancy.reshape(1, VOX), rulebook.reshape(1, 27)
    a, b = call(
        first_kernel,
        (SIDE, SIDE),
        [SMEM] + [ANY] * 3,
        [pltpu.VMEM((VOX, LANES), BF16), pltpu.VMEM((1, VOX), jnp.int32), pltpu.SMEM((1, 27), jnp.int32), SEM((3,))],
        params=ROOMY,
    )(parity, *inputs)
    a, b = swap_a(a), swap_b(b)
    masked, mask, rule, filter_here = call(
        prep_kernel, (BLOCK, WIDE_BLOCK, sds((27, LANES), F32), FILTER), [VMEM] * 4
    )(*inputs, filter_one)
    act_one, act_below, act_above, pre_one = call(
        one_kernel,
        (BLOCK, LAYER, LAYER, WIDE_BLOCK),
        [SMEM] + [VMEM] * 6,
        [WIN_SCRATCH, pltpu.VMEM((128, 27 * LANES), BF16)],
        CONV,
    )(parity, rule, masked, mask, a, b, filter_here)
    win_two, grad_two, small, e, f = call(
        functools.partial(two_kernel, classes),
        (WINDOWS, BLOCK, sds((SMALL, LANES), F32), LAYER, LAYER),
        [SMEM] + [VMEM] * 8,
        flops=CONV,
    )(parity, rule, act_one, act_below, act_above, filter_two, mask, labels.reshape(1, VOX), head_weight.T)
    e, f = swap_a(e), swap_b(f)
    terms_two, win_one = call(terms_kernel, (TERMS, WINDOWS), [SMEM] + [VMEM] * 7, [WIDE_SCRATCH], CONV)(
        parity, rule, masked, a, b, win_two, grad_two, small
    )
    grad_one, terms_one, g, h = call(
        three_kernel,
        (BLOCK, TERMS, LAYER, LAYER),
        [SMEM] + [VMEM] * 9,
        [WIN_SCRATCH, WIDE_SCRATCH],
        2 * CONV,
    )(parity, rule, grad_two, e, f, filter_two, mask, pre_one, win_one, small)
    g, h = swap_a(g), swap_b(h)
    peers = lax.axis_size("near") * lax.axis_size("x")
    rows = -(-27 * LANES // (peers * 16)) * 16
    away = jnp.where(core[0] == 0, terms_two, terms_one)
    chunks = call(
        functools.partial(pair_kernel, rows, peers),
        sds((peers, rows + 2 * SMALL, LANES), BF16),
        [SMEM] + [VMEM] * 3,
    )(core, terms_one, terms_two, core_swap(away))
    parts = lax.all_to_all(chunks, ("near", "x"), 0, 0, tiled=True)
    part = call(
        functools.partial(half_kernel, rows, peers), sds((rows + 2 * SMALL, LANES), BF16), [VMEM]
    )(parts)
    copies, head_sum, loss = call(
        functools.partial(copies_kernel, rows, peers, classes),
        (sds((peers, rows, LANES), BF16), sds((classes, LANES), F32), sds((1, LANES), F32)),
        [VMEM, VMEM, ANY, ANY],
    )(part, far_swap(part), g, h)
    whole = lax.all_to_all(copies, ("near", "x"), 0, 0, tiled=True)
    whole = whole.reshape(peers * rows, LANES)[: 27 * LANES].reshape(27, LANES, LANES)
    whole_other = core_swap(whole)
    grad_in = call(four_kernel, BLOCK, [SMEM] + [VMEM] * 6, [WIN_SCRATCH], CONV)(
        parity, rule, grad_one, g, h, filter_one, mask
    )
    wide = sds((27, LANES, LANES), F32)
    room = [pltpu.VMEM((27, LANES, LANES), F32), SEM((3,))]
    parts = call(own_kernel, (wide, wide), [SMEM, VMEM], room, out_specs=(ANY, ANY))(core, whole)
    sum_one, sum_two = call(
        other_kernel, (wide, wide), [SMEM, VMEM, ANY, ANY], room, out_specs=(ANY, ANY), alias={2: 0, 3: 1}
    )(1 - core, whole_other, *parts)
    return (
        sum_one,
        sum_two,
        head_sum.T,
        loss[0, 0],
        grad_in.reshape(features.shape),
    )


def solution(mesh):
    shape = mesh.devices.shape
    inner = Mesh(mesh.devices.reshape(2, shape[0] // 2, shape[1] // 2, 2), ("far", "near", "x", "core"))
    parts = ("x", "core")
    placed = (
        P(parts, SPACE, None, None),
        P(parts, SPACE, None),
        P(parts, SPACE, None),
        P(parts, SPACE, None),
        P(),
        P(),
        P(),
    )

    def whole(features, occupancy, labels, rulebook, filter_one, filter_two, head_weight):
        step = jax.shard_map(
            functools.partial(local, head_weight.shape[1]),
            mesh=inner,
            in_specs=placed,
            out_specs=(P(), P(), P(), P(), P(parts, SPACE, None, None)),
            check_vma=False,
        )
        return step(features, occupancy, labels, rulebook, filter_one, filter_two, head_weight)

    return whole
```

```python
import functools

import jax
import jax.numpy as jnp
from jax import lax
from jax.experimental import pallas as pl
from jax.experimental.pallas import tpu as pltpu
from jax.sharding import Mesh, PartitionSpec as P

EDGE = 8
VOX = 512
LANES = 128
TAPS = 9
SMALL = 8
SPACE = ("far", "near")
F32 = jnp.float32
BF16 = jnp.bfloat16
PARAMS = pltpu.CompilerParams(vmem_limit_bytes=16 * 1024 * 1024)
ROOMY = pltpu.CompilerParams(vmem_limit_bytes=62 * 1024 * 1024)
VMEM = pl.BlockSpec(memory_space=pltpu.VMEM)
ANY = pl.BlockSpec(memory_space=pl.ANY)
SMEM = pl.BlockSpec(memory_space=pltpu.SMEM)


def sds(shape, dtype):
    return jax.ShapeDtypeStruct(shape, dtype)


def contract(a, b, dim_a, dim_b):
    return lax.dot_general(a, b, (((dim_a,), (dim_b,)), ((), ())), preferred_element_type=F32)


def spread_layer(layer):
    return jnp.broadcast_to(layer.astype(F32).reshape(64, 1, LANES), (64, EDGE, LANES))


def from_sides(parity_ref, recv_a, recv_b):
    even = parity_ref[0] == 0
    got_a, got_b = recv_a.astype(F32), recv_b.astype(F32)
    return jnp.where(even, got_b, got_a), jnp.where(even, got_a, got_b)


def build_windows(block, below, above, rule_ref, out_ref):
    cells = block.reshape(64, EDGE, LANES)
    depth = lax.broadcasted_iota(jnp.int32, (1, EDGE, LANES), 1)

    def flag(i, j, k, wanted):
        offset = 9 * i + 3 * j + k
        return jnp.where(rule_ref[offset : offset + 1, :] == wanted, 1.0, 0.0).reshape(1, 1, LANES)

    for k in range(3):
        if k == 1:
            own, other = cells, None
        elif k == 0:
            own, other = pltpu.roll(cells, 1, 1), spread_layer(below)
        else:
            own, other = pltpu.roll(cells, EDGE - 1, 1), spread_layer(above)
        own = own.reshape(EDGE, EDGE, EDGE, LANES)
        if other is not None:
            other = other.reshape(EDGE, EDGE, EDGE, LANES)

        def region(i, j):
            xs = {0: slice(7, 8), 1: slice(0, 8), 2: slice(0, 1)}[i]
            ys = {0: slice(7, 8), 1: slice(0, 8), 2: slice(0, 1)}[j]
            inner = flag(i, j, 1, 0)
            if k == 1:
                return own[xs, ys] * inner[None]
            edge = depth == (0 if k == 0 else EDGE - 1)
            keep = jnp.where(edge, flag(i, j, k, 0), inner)
            take = jnp.where(edge, flag(i, j, k, 1 if k == 0 else 2), 0.0)
            return own[xs, ys] * keep[None] + other[xs, ys] * take[None]

        columns = [jnp.concatenate([region(i, j) for i in range(3)], axis=0).astype(F32) for j in range(3)]
        for j in range(3):
            if j == 0:
                padded = jnp.concatenate([columns[0], columns[1][:, :7]], axis=1)
            elif j == 1:
                padded = columns[1]
            else:
                padded = jnp.concatenate([columns[1][:, 1:], columns[2]], axis=1)
            lane = (3 * j + k) * LANES
            out_ref[:, lane : lane + LANES] = padded.reshape(640, LANES).astype(BF16)


def put_sides(parity_ref, upward, downward, send_a_ref, send_b_ref):
    even = parity_ref[0] == 0
    send_a_ref[...] = jnp.where(even, upward, downward).astype(BF16)
    send_b_ref[...] = jnp.where(even, downward, upward).astype(BF16)


def layers_of(block):
    cells = block.reshape(64, EDGE, LANES)
    return lambda z: cells[:, z, :]


def put_layers(block, parity_ref, send_a_ref, send_b_ref):
    layer = layers_of(block)
    put_sides(parity_ref, layer(EDGE - 1), layer(0), send_a_ref, send_b_ref)


def layer_windows(side, mine, touching, rule, out_ref, row):
    near, behind, wrap = (part.reshape(EDGE, EDGE, LANES) for part in side)
    mine = mine.reshape(EDGE, EDGE, LANES)
    across = 2 if touching == EDGE - 1 else 0
    width = lax.broadcasted_iota(jnp.int32, (1, EDGE, LANES), 1)

    def flag(i, j, k, wanted):
        offset = 9 * i + 3 * j + k
        return jnp.where(rule[offset : offset + 1, :] == wanted, 1.0, 0.0).reshape(1, 1, LANES)

    for k in range(3):
        sources = [(near if k == 1 else behind, 1, 0)]
        if k == across:
            sources = [(wrap, k, 0), (mine, k, 2 if across == 2 else 1)]
        for j in range(3):
            base = first = last = None
            for layer, region, wanted in sources:
                turned = layer if j == 1 else pltpu.roll(layer, 1 if j == 0 else EDGE - 1, 1)

                def gate(i):
                    inner = flag(i, 1, region, wanted)
                    if j == 1:
                        return inner
                    return jnp.where(width == (0 if j == 0 else EDGE - 1), flag(i, j, region, wanted), inner)

                parts = turned * gate(1), turned[7:8] * gate(0), turned[0:1] * gate(2)
                if base is None:
                    base, first, last = parts
                else:
                    base, first, last = base + parts[0], first + parts[1], last + parts[2]
            for i in range(3):
                cells = base
                if i == 0:
                    cells = jnp.concatenate([first, base[:7]], axis=0)
                elif i == 2:
                    cells = jnp.concatenate([base[1:], last], axis=0)
                lane = (9 * i + 3 * j + k) * LANES
                out_ref[row : row + 64, lane : lane + LANES] = cells.reshape(64, LANES).astype(BF16)


def forward_sum(win_ref, filt_ref):
    total = None
    for i in range(3):
        filt = filt_ref[TAPS * i : TAPS * (i + 1)].reshape(TAPS * LANES, LANES)
        term = jnp.dot(win_ref[64 * i : 64 * i + VOX, :], filt, preferred_element_type=F32)
        total = term if total is None else total + term
    return total


def backward_sum(win_ref, filt_ref):
    total = None
    for i in range(3):
        filt = jnp.concatenate([filt_ref[26 - TAPS * i - t] for t in range(TAPS)], axis=1)
        term = contract(win_ref[64 * i : 64 * i + VOX, :], filt, 1, 1)
        total = term if total is None else total + term
    return total


def filter_terms(win_ref, grad, core_ref, wide_ref, tiles_ref, mine_ref, away_ref):
    wide_ref[...] = jnp.zeros_like(wide_ref)
    for i in range(3):
        wide_ref[64 * i : 64 * i + VOX, LANES * i : LANES * (i + 1)] = grad
    for t in range(TAPS):
        term = contract(win_ref[:, LANES * t : LANES * (t + 1)], wide_ref[...], 0, 0)
        for i in range(3):
            tile = term[:, LANES * i : LANES * (i + 1)].astype(BF16)
            at = 2 * (TAPS * i + t)
            tiles_ref[at // 27, at % 27] = tile[:64]
            tiles_ref[(at + 1) // 27, (at + 1) % 27] = tile[64:]
    core = core_ref[0]
    mine_ref[:27] = tiles_ref[core]
    away_ref[:27] = tiles_ref[1 - core]


def silu_parts(pre):
    sigmoid = 1.0 / (1.0 + jnp.exp(-pre))
    return pre * sigmoid, sigmoid * (1.0 + pre * (1.0 - sigmoid))


def filled_rows(occ):
    rows = lax.broadcasted_iota(jnp.int32, (SMALL, VOX), 0)
    occ_rows = jnp.where(rows == 0, jnp.broadcast_to(occ, (SMALL, VOX)), 0).astype(F32).astype(BF16)
    row = lax.broadcasted_iota(jnp.int32, (SMALL, LANES), 0)
    return contract(occ_rows, jnp.where(row == 0, 1.0, 0.0).astype(BF16), 0, 0)


def first_kernel(parity, feat_hbm, occ_hbm, rule_hbm, send_a, send_b, feat, occ, rule, sems):
    copies = [
        pltpu.make_async_copy(feat_hbm, feat, sems.at[0]),
        pltpu.make_async_copy(occ_hbm, occ, sems.at[1]),
        pltpu.make_async_copy(rule_hbm, rule, sems.at[2]),
    ]
    for copy in copies:
        copy.start()
    for copy in copies:
        copy.wait()
    filled = filled_rows(occ[...])
    block = feat[...].astype(F32) * filled
    offsets = lax.broadcasted_iota(jnp.int32, (32, LANES), 0)
    found = jnp.zeros((32, LANES), jnp.int32)
    for o in range(27):
        found = jnp.where(offsets == o, rule[0, o], found)
    found = found.astype(F32)
    layer, held = layers_of(block), layers_of(filled)
    top = EDGE - 1
    upward = jnp.concatenate([layer(top), layer(top - 1), layer(0), held(top), found], axis=0)
    downward = jnp.concatenate([layer(0), layer(1), layer(top), held(0), found], axis=0)
    put_sides(parity, upward, downward, send_a, send_b)


def prep_kernel(feat, occ, found, filt_in, masked, mask, rule, filt):
    filt[...] = filt_in[...]
    row = lax.broadcasted_iota(jnp.int32, (SMALL, 27), 0)
    rule_rows = jnp.where(row == 0, jnp.broadcast_to(found[...], (SMALL, 27)), 0).astype(F32).astype(BF16)
    one_row = lax.broadcasted_iota(jnp.int32, (SMALL, LANES), 0)
    rule[...] = contract(rule_rows, jnp.where(one_row == 0, 1.0, 0.0).astype(BF16), 0, 0)
    filled = filled_rows(occ[...])
    mask[...] = filled
    masked[...] = (feat[...].astype(F32) * filled).astype(BF16)


def one_kernel(parity, rule, masked, mask, recv_a, recv_b, filt, act, act_below, act_above, pre, win, rim):
    below, above = from_sides(parity, recv_a[...], recv_b[...])
    block = masked[...].astype(F32)
    build_windows(block, below[:64], above[:64], rule, win)
    total = forward_sum(win, filt) * mask[...]
    pre[...] = total
    acted, _ = silu_parts(total)
    act[...] = acted.astype(BF16)
    layer = layers_of(block)
    for side, mine, touching, row in ((below, layer(0), EDGE - 1, 0), (above, layer(EDGE - 1), 0, 64)):
        parts = [side[at : at + 64] for at in (0, 64, 128)]
        layer_windows(parts, mine, touching, side[256:288], rim, row)
    total = None
    wide = TAPS * LANES
    for i in range(3):
        weights = filt[TAPS * i : TAPS * (i + 1)].reshape(wide, LANES)
        term = jnp.dot(rim[:, wide * i : wide * (i + 1)], weights, preferred_element_type=F32)
        total = term if total is None else total + term
    for side, row, out in ((below, 0, act_below), (above, 64, act_above)):
        acted, _ = silu_parts(total[row : row + 64] * side[192:256])
        out[...] = acted.astype(BF16)


def two_kernel(
    classes, parity, rule, act_one, act_below, act_above, filt, mask, labels, head_rows,
    win, grad, small, send_a, send_b,
):
    build_windows(act_one[...].astype(F32), act_below[...].astype(F32), act_above[...].astype(F32), rule, win)
    head = jnp.concatenate([head_rows[...].astype(F32), jnp.zeros((LANES - classes, LANES), F32)], axis=0).astype(BF16)
    rows = lax.broadcasted_iota(jnp.int32, (SMALL, VOX), 0)
    hot_rows = jnp.where(rows == jnp.broadcast_to(labels[...], (SMALL, VOX)), 1.0, 0.0).astype(BF16)
    unit_row = lax.broadcasted_iota(jnp.int32, (SMALL, LANES), 0)
    unit_lane = lax.broadcasted_iota(jnp.int32, (SMALL, LANES), 1)
    hot = contract(hot_rows, jnp.where(unit_row == unit_lane, 1.0, 0.0).astype(BF16), 0, 0)
    filled = mask[...]
    pre = forward_sum(win, filt) * filled
    acted, slope = silu_parts(pre)
    acted = acted.astype(BF16)
    lane = lax.broadcasted_iota(jnp.int32, (VOX, LANES), 1)
    logits = contract(acted, head, 1, 1)
    known = lane < classes
    top = jnp.max(jnp.where(known, logits, -jnp.inf), axis=1, keepdims=True)
    powers = jnp.where(known, jnp.exp(jnp.where(known, logits - top, 0.0)), 0.0)
    total_log = top + jnp.log(jnp.sum(powers, axis=1, keepdims=True))
    chances = jnp.where(known, jnp.exp(jnp.where(known, logits - total_log, 0.0)), 0.0)
    dlogits = (chances - hot) * filled
    high = dlogits.astype(BF16)
    low = (dlogits - high.astype(F32)).astype(BF16)
    back = jnp.dot(high, head, preferred_element_type=F32) + jnp.dot(low, head, preferred_element_type=F32)
    out = (back * slope * filled).astype(BF16)
    grad[...] = out
    put_layers(out.astype(F32), parity, send_a, send_b)
    head_terms = (contract(high, acted, 0, 0) + contract(low, acted, 0, 0))[:SMALL]
    losses = jnp.sum((total_log - logits) * hot * filled, axis=0, keepdims=True)
    counted = jnp.sum(filled, axis=0, keepdims=True)
    tail = jnp.where(lane[:1] < classes, losses, jnp.where(lane[:1] == classes, counted, 0.0))
    row = lax.broadcasted_iota(jnp.int32, (SMALL, LANES), 0)
    values = jnp.where(row < classes, head_terms, jnp.where(row == classes, tail, 0.0))
    small[...] = values


def terms_kernel(
    core, parity, rule, masked, recv_a, recv_b, win_two, grad, small, mine, away, win_one, wide, tiles
):
    filter_terms(win_two, grad[...], core, wide, tiles, mine, away)
    pair = jnp.concatenate([split_pair(small[: SMALL // 2]), jnp.zeros((64 - SMALL, LANES), F32)], axis=0).astype(BF16)
    mine[27], away[27] = pair, pair
    below, above = from_sides(parity, recv_a[...], recv_b[...])
    build_windows(masked[...].astype(F32), below[:64], above[:64], rule, win_one)


def three_kernel(
    core, parity, rule, grad_two, recv_a, recv_b, filt, mask, pre, win_one,
    grad_one, mine, away, send_a, send_b, win, wide, tiles,
):
    below, above = from_sides(parity, recv_a[...], recv_b[...])
    build_windows(grad_two[...].astype(F32), below, above, rule, win)
    _, slope = silu_parts(pre[...])
    out = (backward_sum(win, filt) * slope * mask[...]).astype(BF16)
    grad_one[...] = out
    put_layers(out.astype(F32), parity, send_a, send_b)
    filter_terms(win_one, out, core, wide, tiles, mine, away)


def four_kernel(parity, rule, grad_one, recv_a, recv_b, filt, mask, out, win):
    below, above = from_sides(parity, recv_a[...], recv_b[...])
    build_windows(grad_one[...].astype(F32), below, above, rule, win)
    total = backward_sum(win, filt) * mask[...]
    out[...] = total.astype(BF16)


def own_kernel(core, whole, one, two, wide, sems):
    copies = []
    for layer, out in enumerate((one, two)):
        for part in range(3):
            at = pl.ds(TAPS * part, TAPS)
            wide[layer, at] = whole[layer, at].astype(F32) * (1.0 / VOX)
            copies.append(pltpu.make_async_copy(wide.at[layer, at], out.at[core[0], at], sems.at[3 * layer + part]))
            copies[-1].start()
    for copy in copies:
        copy.wait()


def other_kernel(core, whole, one_in, two_in, one, two, wide, sems):
    own_kernel(core, whole, one, two, wide, sems)


def call(kernel, outs, specs, scratch=(), flops=0, params=PARAMS, out_specs=None, alias=None):
    return pl.pallas_call(
        kernel,
        out_shape=outs,
        in_specs=specs,
        out_specs=jax.tree.map(lambda _: VMEM, outs) if out_specs is None else out_specs,
        input_output_aliases=alias or {},
        scratch_shapes=list(scratch),
        compiler_params=params,
        cost_estimate=pl.CostEstimate(flops=flops, bytes_accessed=4_000_000, transcendentals=0),
    )


BLOCK = sds((VOX, LANES), BF16)
WIDE_BLOCK = sds((VOX, LANES), F32)
LAYER = sds((64, LANES), BF16)
FILTER = sds((27, LANES, LANES), BF16)
SIDE = sds((288, LANES), BF16)
WINDOWS = sds((640, TAPS * LANES), BF16)
TERMS = sds((27, 64, LANES), BF16)
GIVEN = sds((28, 64, LANES), BF16)
TILES_SCRATCH = pltpu.VMEM((2, 27, 64, LANES), BF16)
WIN_SCRATCH = pltpu.VMEM((640, TAPS * LANES), BF16)
SEM = pltpu.SemaphoreType.DMA
WIDE_SCRATCH = pltpu.VMEM((640, 3 * LANES), BF16)
CONV = 2 * 27 * VOX * LANES * LANES


def swap_a(value):
    length = lax.axis_size(SPACE)
    return lax.ppermute(value, SPACE, [(i, i ^ 1) for i in range(length)])


def swap_b(value):
    length = lax.axis_size(SPACE)
    pairs = []
    for i in range(length):
        to = i + 1 if i % 2 else i - 1
        for c in range(2):
            pairs.append((2 * i + c, 2 * to + c if 0 <= to < length else 2 * i + 1 - c))
    return lax.ppermute(value, SPACE + ("core",), pairs)


def far_swap(value):
    return lax.ppermute(value, "far", [(0, 1), (1, 0)])


def core_swap(value):
    return lax.ppermute(value, "core", [(0, 1), (1, 0)])


def split_pair(value):
    high = value.astype(BF16).astype(F32)
    return jnp.concatenate([high, value - high], axis=0)


def join_pair(pair):
    return pair[: SMALL // 2] + pair[SMALL // 2 : SMALL]


def pair_kernel(rows, peers, one, one_other, two, two_other, out):
    small = join_pair(two[27].astype(F32)) + join_pair(two_other[27].astype(F32))
    tail = jnp.concatenate([split_pair(small), jnp.zeros((SMALL, LANES), F32)], axis=0)
    halves = [
        a[:27].reshape(27 * 64, LANES).astype(F32) + b[:27].reshape(27 * 64, LANES).astype(F32)
        for a, b in ((one, one_other), (two, two_other))
    ]
    total = jnp.concatenate(halves, axis=0)
    spare = rows * peers - 27 * LANES
    if spare:
        total = jnp.concatenate([total, jnp.zeros((spare, LANES), F32)], axis=0)
    for p in range(peers):
        out[p] = jnp.concatenate([total[p * rows : (p + 1) * rows], tail], axis=0).astype(BF16)


def half_kernel(rows, peers, parts, out):
    total = parts[0].astype(F32)
    for p in range(1, peers):
        total = total + parts[p].astype(F32)
    tail = split_pair(join_pair(total[rows : rows + SMALL]))
    out[...] = jnp.concatenate([total[:rows], tail, jnp.zeros((SMALL, LANES), F32)], axis=0).astype(BF16)


def copies_kernel(rows, peers, classes, mine, other, later_a, later_b, out, head, loss):
    a, b = mine[...].astype(F32), other[...].astype(F32)
    both = (a[:rows] + b[:rows]).astype(BF16)
    for p in range(peers):
        out[p] = both
    tail = join_pair(a[rows:]) + join_pair(b[rows:])
    head[...] = tail[:classes] * (1.0 / VOX)
    last = tail[classes : classes + 1]
    lane = lax.broadcasted_iota(jnp.int32, (1, LANES), 1)
    losses = jnp.sum(jnp.where(lane < classes, last, 0.0), axis=1, keepdims=True)
    counted = jnp.sum(jnp.where(lane == classes, last, 0.0), axis=1, keepdims=True)
    loss[...] = jnp.broadcast_to(losses / counted, (1, LANES))


def local(classes, features, occupancy, labels, rulebook, filter_one, filter_two, head_weight):
    parity = (lax.axis_index(SPACE) % 2).reshape(1).astype(jnp.int32)
    core = lax.axis_index("core").reshape(1).astype(jnp.int32)
    inputs = features.reshape(VOX, LANES), occupancy.reshape(1, VOX), rulebook.reshape(1, 27)
    a, b = call(
        first_kernel,
        (SIDE, SIDE),
        [SMEM] + [ANY] * 3,
        [pltpu.VMEM((VOX, LANES), BF16), pltpu.VMEM((1, VOX), jnp.int32), pltpu.SMEM((1, 27), jnp.int32), SEM((3,))],
        params=ROOMY,
    )(parity, *inputs)
    a, b = swap_a(a), swap_b(b)
    masked, mask, rule, filter_here = call(
        prep_kernel, (BLOCK, WIDE_BLOCK, sds((27, LANES), F32), FILTER), [VMEM] * 4
    )(*inputs, filter_one)
    act_one, act_below, act_above, pre_one = call(
        one_kernel,
        (BLOCK, LAYER, LAYER, WIDE_BLOCK),
        [SMEM] + [VMEM] * 6,
        [WIN_SCRATCH, pltpu.VMEM((128, 27 * LANES), BF16)],
        CONV,
    )(parity, rule, masked, mask, a, b, filter_here)
    win_two, grad_two, small, e, f = call(
        functools.partial(two_kernel, classes),
        (WINDOWS, BLOCK, sds((SMALL, LANES), F32), LAYER, LAYER),
        [SMEM] + [VMEM] * 8,
        flops=CONV,
    )(parity, rule, act_one, act_below, act_above, filter_two, mask, labels.reshape(1, VOX), head_weight.T)
    e, f = swap_a(e), swap_b(f)
    mine_two, away_two, win_one = call(
        terms_kernel, (GIVEN, GIVEN, WINDOWS), [SMEM] * 2 + [VMEM] * 7, [WIDE_SCRATCH, TILES_SCRATCH], CONV
    )(core, parity, rule, masked, a, b, win_two, grad_two, small)
    other_two = core_swap(away_two)
    grad_one, mine_one, away_one, g, h = call(
        three_kernel,
        (BLOCK, TERMS, TERMS, LAYER, LAYER),
        [SMEM] * 2 + [VMEM] * 8,
        [WIN_SCRATCH, WIDE_SCRATCH, TILES_SCRATCH],
        2 * CONV,
    )(core, parity, rule, grad_two, e, f, filter_two, mask, pre_one, win_one)
    g, h = swap_a(g), swap_b(h)
    peers = lax.axis_size("near") * lax.axis_size("x")
    rows = -(-27 * LANES // (peers * 16)) * 16
    chunks = call(
        functools.partial(pair_kernel, rows, peers), sds((peers, rows + 2 * SMALL, LANES), BF16), [VMEM] * 4
    )(mine_one, core_swap(away_one), mine_two, other_two)
    parts = lax.all_to_all(chunks, ("near", "x"), 0, 0, tiled=True)
    part = call(
        functools.partial(half_kernel, rows, peers), sds((rows + 2 * SMALL, LANES), BF16), [VMEM]
    )(parts)
    copies, head_sum, loss = call(
        functools.partial(copies_kernel, rows, peers, classes),
        (sds((peers, rows, LANES), BF16), sds((classes, LANES), F32), sds((1, LANES), F32)),
        [VMEM, VMEM, ANY, ANY],
    )(part, far_swap(part), g, h)
    whole = lax.all_to_all(copies, ("near", "x"), 0, 0, tiled=True)
    whole = whole.reshape(peers * rows, LANES)[: 27 * LANES].reshape(2, 27, 64, LANES)
    whole_other = core_swap(whole)
    grad_in = call(four_kernel, BLOCK, [SMEM] + [VMEM] * 6, [WIN_SCRATCH], CONV)(
        parity, rule, grad_one, g, h, filter_one, mask
    )
    wide = sds((2, 27, 64, LANES), F32)
    room = [pltpu.VMEM((2, 27, 64, LANES), F32), SEM((6,))]
    parts = call(own_kernel, (wide, wide), [SMEM, VMEM], room, out_specs=(ANY, ANY))(core, whole)
    sum_one, sum_two = call(
        other_kernel, (wide, wide), [SMEM, VMEM, ANY, ANY], room, out_specs=(ANY, ANY), alias={2: 0, 3: 1}
    )(1 - core, whole_other, *parts)
    return (
        sum_one.reshape(27, LANES, LANES),
        sum_two.reshape(27, LANES, LANES),
        head_sum.T,
        loss[0, 0],
        grad_in.reshape(features.shape),
    )


def solution(mesh):
    shape = mesh.devices.shape
    inner = Mesh(mesh.devices.reshape(2, shape[0] // 2, shape[1] // 2, 2), ("far", "near", "x", "core"))
    parts = ("x", "core")
    placed = (
        P(parts, SPACE, None, None),
        P(parts, SPACE, None),
        P(parts, SPACE, None),
        P(parts, SPACE, None),
        P(),
        P(),
        P(),
    )

    def whole(features, occupancy, labels, rulebook, filter_one, filter_two, head_weight):
        step = jax.shard_map(
            functools.partial(local, head_weight.shape[1]),
            mesh=inner,
            in_specs=placed,
            out_specs=(P(), P(), P(), P(), P(parts, SPACE, None, None)),
            check_vma=False,
        )
        return step(features, occupancy, labels, rulebook, filter_one, filter_two, head_weight)

    return whole
```

```python
import functools

import jax
import jax.numpy as jnp
from jax import lax
from jax.experimental import pallas as pl
from jax.experimental.pallas import tpu as pltpu
from jax.sharding import Mesh, PartitionSpec as P

EDGE = 8
VOX = 512
LANES = 128
TAPS = 9
SMALL = 8
SPACE = ("far", "near")
F32 = jnp.float32
BF16 = jnp.bfloat16
PARAMS = pltpu.CompilerParams(vmem_limit_bytes=16 * 1024 * 1024)
ROOMY = pltpu.CompilerParams(vmem_limit_bytes=62 * 1024 * 1024)
VMEM = pl.BlockSpec(memory_space=pltpu.VMEM)
ANY = pl.BlockSpec(memory_space=pl.ANY)
SMEM = pl.BlockSpec(memory_space=pltpu.SMEM)


def sds(shape, dtype):
    return jax.ShapeDtypeStruct(shape, dtype)


def contract(a, b, dim_a, dim_b):
    return lax.dot_general(a, b, (((dim_a,), (dim_b,)), ((), ())), preferred_element_type=F32)


def spread_layer(layer):
    return jnp.broadcast_to(layer.astype(F32).reshape(64, 1, LANES), (64, EDGE, LANES))


def from_sides(parity_ref, recv_a, recv_b):
    even = parity_ref[0] == 0
    got_a, got_b = recv_a.astype(F32), recv_b.astype(F32)
    return jnp.where(even, got_b, got_a), jnp.where(even, got_a, got_b)


def build_windows(block, below, above, rule_ref, out_ref):
    cells = block.reshape(64, EDGE, LANES)
    depth = lax.broadcasted_iota(jnp.int32, (1, EDGE, LANES), 1)

    def flag(i, j, k, wanted):
        offset = 9 * i + 3 * j + k
        return jnp.where(rule_ref[offset : offset + 1, :] == wanted, 1.0, 0.0).reshape(1, 1, LANES)

    for k in range(3):
        if k == 1:
            own, other = cells, None
        elif k == 0:
            own, other = pltpu.roll(cells, 1, 1), spread_layer(below)
        else:
            own, other = pltpu.roll(cells, EDGE - 1, 1), spread_layer(above)
        own = own.reshape(EDGE, EDGE, EDGE, LANES)
        if other is not None:
            other = other.reshape(EDGE, EDGE, EDGE, LANES)

        def region(i, j):
            xs = {0: slice(7, 8), 1: slice(0, 8), 2: slice(0, 1)}[i]
            ys = {0: slice(7, 8), 1: slice(0, 8), 2: slice(0, 1)}[j]
            inner = flag(i, j, 1, 0)
            if k == 1:
                return own[xs, ys] * inner[None]
            edge = depth == (0 if k == 0 else EDGE - 1)
            keep = jnp.where(edge, flag(i, j, k, 0), inner)
            take = jnp.where(edge, flag(i, j, k, 1 if k == 0 else 2), 0.0)
            return own[xs, ys] * keep[None] + other[xs, ys] * take[None]

        columns = [jnp.concatenate([region(i, j) for i in range(3)], axis=0).astype(F32) for j in range(3)]
        for j in range(3):
            if j == 0:
                padded = jnp.concatenate([columns[0], columns[1][:, :7]], axis=1)
            elif j == 1:
                padded = columns[1]
            else:
                padded = jnp.concatenate([columns[1][:, 1:], columns[2]], axis=1)
            lane = (3 * j + k) * LANES
            out_ref[:, lane : lane + LANES] = padded.reshape(640, LANES).astype(BF16)


def put_sides(parity_ref, upward, downward, send_a_ref, send_b_ref):
    even = parity_ref[0] == 0
    send_a_ref[...] = jnp.where(even, upward, downward).astype(BF16)
    send_b_ref[...] = jnp.where(even, downward, upward).astype(BF16)


def layers_of(block):
    cells = block.reshape(64, EDGE, LANES)
    return lambda z: cells[:, z, :]


def put_layers(block, parity_ref, send_a_ref, send_b_ref):
    layer = layers_of(block)
    put_sides(parity_ref, layer(EDGE - 1), layer(0), send_a_ref, send_b_ref)


def layer_windows(side, mine, touching, rule, out_ref, row):
    near, behind, wrap = (part.reshape(EDGE, EDGE, LANES) for part in side)
    mine = mine.reshape(EDGE, EDGE, LANES)
    across = 2 if touching == EDGE - 1 else 0
    width = lax.broadcasted_iota(jnp.int32, (1, EDGE, LANES), 1)

    def flag(i, j, k, wanted):
        offset = 9 * i + 3 * j + k
        return jnp.where(rule[offset : offset + 1, :] == wanted, 1.0, 0.0).reshape(1, 1, LANES)

    for k in range(3):
        sources = [(near if k == 1 else behind, 1, 0)]
        if k == across:
            sources = [(wrap, k, 0), (mine, k, 2 if across == 2 else 1)]
        for j in range(3):
            base = first = last = None
            for layer, region, wanted in sources:
                turned = layer if j == 1 else pltpu.roll(layer, 1 if j == 0 else EDGE - 1, 1)

                def gate(i):
                    inner = flag(i, 1, region, wanted)
                    if j == 1:
                        return inner
                    return jnp.where(width == (0 if j == 0 else EDGE - 1), flag(i, j, region, wanted), inner)

                parts = turned * gate(1), turned[7:8] * gate(0), turned[0:1] * gate(2)
                if base is None:
                    base, first, last = parts
                else:
                    base, first, last = base + parts[0], first + parts[1], last + parts[2]
            for i in range(3):
                cells = base
                if i == 0:
                    cells = jnp.concatenate([first, base[:7]], axis=0)
                elif i == 2:
                    cells = jnp.concatenate([base[1:], last], axis=0)
                lane = (9 * i + 3 * j + k) * LANES
                out_ref[row : row + 64, lane : lane + LANES] = cells.reshape(64, LANES).astype(BF16)


def shifted_sum(wide):
    return sum(wide[64 * i : 64 * i + VOX, LANES * i : LANES * (i + 1)] for i in range(3))


def forward_sum(win_ref, filt_ref):
    parts = [filt_ref[TAPS * i : TAPS * (i + 1)].reshape(TAPS * LANES, LANES) for i in range(3)]
    return shifted_sum(jnp.dot(win_ref[...], jnp.concatenate(parts, axis=1), preferred_element_type=F32))


def backward_sum(win_ref, filt_ref):
    parts = [jnp.concatenate([filt_ref[26 - TAPS * i - t] for t in range(TAPS)], axis=1) for i in range(3)]
    return shifted_sum(contract(win_ref[...], jnp.concatenate(parts, axis=0), 1, 1))


def filter_terms(win_ref, grad, core_ref, wide_ref, tiles_ref, mine_ref, away_ref):
    wide_ref[...] = jnp.zeros_like(wide_ref)
    for i in range(3):
        wide_ref[64 * i : 64 * i + VOX, LANES * i : LANES * (i + 1)] = grad
    for t in range(TAPS):
        term = contract(win_ref[:, LANES * t : LANES * (t + 1)], wide_ref[...], 0, 0)
        for i in range(3):
            tile = term[:, LANES * i : LANES * (i + 1)].astype(BF16)
            at = 2 * (TAPS * i + t)
            tiles_ref[at // 27, at % 27] = tile[:64]
            tiles_ref[(at + 1) // 27, (at + 1) % 27] = tile[64:]
    core = core_ref[0]
    mine_ref[:27] = tiles_ref[core]
    away_ref[:27] = tiles_ref[1 - core]


def silu_parts(pre):
    sigmoid = 1.0 / (1.0 + jnp.exp(-pre))
    return pre * sigmoid, sigmoid * (1.0 + pre * (1.0 - sigmoid))


def filled_rows(occ):
    rows = lax.broadcasted_iota(jnp.int32, (SMALL, VOX), 0)
    occ_rows = jnp.where(rows == 0, jnp.broadcast_to(occ, (SMALL, VOX)), 0).astype(F32).astype(BF16)
    row = lax.broadcasted_iota(jnp.int32, (SMALL, LANES), 0)
    return contract(occ_rows, jnp.where(row == 0, 1.0, 0.0).astype(BF16), 0, 0)


def first_kernel(parity, feat_hbm, occ_hbm, rule_hbm, send_a, send_b, feat, occ, rule, sems):
    copies = [
        pltpu.make_async_copy(feat_hbm, feat, sems.at[0]),
        pltpu.make_async_copy(occ_hbm, occ, sems.at[1]),
        pltpu.make_async_copy(rule_hbm, rule, sems.at[2]),
    ]
    for copy in copies:
        copy.start()
    for copy in copies:
        copy.wait()
    filled = filled_rows(occ[...])
    block = feat[...].astype(F32) * filled
    offsets = lax.broadcasted_iota(jnp.int32, (32, LANES), 0)
    found = jnp.zeros((32, LANES), jnp.int32)
    for o in range(27):
        found = jnp.where(offsets == o, rule[0, o], found)
    found = found.astype(F32)
    layer, held = layers_of(block), layers_of(filled)
    top = EDGE - 1
    upward = jnp.concatenate([layer(top), layer(top - 1), layer(0), held(top), found], axis=0)
    downward = jnp.concatenate([layer(0), layer(1), layer(top), held(0), found], axis=0)
    put_sides(parity, upward, downward, send_a, send_b)


def prep_kernel(feat, occ, found, filt_in, masked, mask, rule, filt):
    filt[...] = filt_in[...]
    row = lax.broadcasted_iota(jnp.int32, (SMALL, 27), 0)
    rule_rows = jnp.where(row == 0, jnp.broadcast_to(found[...], (SMALL, 27)), 0).astype(F32).astype(BF16)
    one_row = lax.broadcasted_iota(jnp.int32, (SMALL, LANES), 0)
    rule[...] = contract(rule_rows, jnp.where(one_row == 0, 1.0, 0.0).astype(BF16), 0, 0)
    filled = filled_rows(occ[...])
    mask[...] = filled
    masked[...] = (feat[...].astype(F32) * filled).astype(BF16)


def one_kernel(parity, rule, masked, mask, recv_a, recv_b, filt, act, act_below, act_above, pre, win, rim):
    below, above = from_sides(parity, recv_a[...], recv_b[...])
    block = masked[...].astype(F32)
    build_windows(block, below[:64], above[:64], rule, win)
    total = forward_sum(win, filt) * mask[...]
    pre[...] = total
    acted, _ = silu_parts(total)
    act[...] = acted.astype(BF16)
    layer = layers_of(block)
    for side, mine, touching, row in ((below, layer(0), EDGE - 1, 0), (above, layer(EDGE - 1), 0, 64)):
        parts = [side[at : at + 64] for at in (0, 64, 128)]
        layer_windows(parts, mine, touching, side[256:288], rim, row)
    total = None
    wide = TAPS * LANES
    for i in range(3):
        weights = filt[TAPS * i : TAPS * (i + 1)].reshape(wide, LANES)
        term = jnp.dot(rim[:, wide * i : wide * (i + 1)], weights, preferred_element_type=F32)
        total = term if total is None else total + term
    for side, row, out in ((below, 0, act_below), (above, 64, act_above)):
        acted, _ = silu_parts(total[row : row + 64] * side[192:256])
        out[...] = acted.astype(BF16)


def two_kernel(
    classes, parity, rule, act_one, act_below, act_above, filt, mask, labels, head_rows,
    win, grad, small, send_a, send_b,
):
    build_windows(act_one[...].astype(F32), act_below[...].astype(F32), act_above[...].astype(F32), rule, win)
    head = jnp.concatenate([head_rows[...].astype(F32), jnp.zeros((LANES - classes, LANES), F32)], axis=0).astype(BF16)
    rows = lax.broadcasted_iota(jnp.int32, (SMALL, VOX), 0)
    hot_rows = jnp.where(rows == jnp.broadcast_to(labels[...], (SMALL, VOX)), 1.0, 0.0).astype(BF16)
    unit_row = lax.broadcasted_iota(jnp.int32, (SMALL, LANES), 0)
    unit_lane = lax.broadcasted_iota(jnp.int32, (SMALL, LANES), 1)
    hot = contract(hot_rows, jnp.where(unit_row == unit_lane, 1.0, 0.0).astype(BF16), 0, 0)
    filled = mask[...]
    pre = forward_sum(win, filt) * filled
    acted, slope = silu_parts(pre)
    acted = acted.astype(BF16)
    lane = lax.broadcasted_iota(jnp.int32, (VOX, LANES), 1)
    logits = contract(acted, head, 1, 1)
    known = lane < classes
    top = jnp.max(jnp.where(known, logits, -jnp.inf), axis=1, keepdims=True)
    powers = jnp.where(known, jnp.exp(jnp.where(known, logits - top, 0.0)), 0.0)
    total_log = top + jnp.log(jnp.sum(powers, axis=1, keepdims=True))
    chances = jnp.where(known, jnp.exp(jnp.where(known, logits - total_log, 0.0)), 0.0)
    dlogits = (chances - hot) * filled
    high = dlogits.astype(BF16)
    low = (dlogits - high.astype(F32)).astype(BF16)
    back = jnp.dot(high, head, preferred_element_type=F32) + jnp.dot(low, head, preferred_element_type=F32)
    out = (back * slope * filled).astype(BF16)
    grad[...] = out
    put_layers(out.astype(F32), parity, send_a, send_b)
    head_terms = (contract(high, acted, 0, 0) + contract(low, acted, 0, 0))[:SMALL]
    losses = jnp.sum((total_log - logits) * hot * filled, axis=0, keepdims=True)
    counted = jnp.sum(filled, axis=0, keepdims=True)
    tail = jnp.where(lane[:1] < classes, losses, jnp.where(lane[:1] == classes, counted, 0.0))
    row = lax.broadcasted_iota(jnp.int32, (SMALL, LANES), 0)
    values = jnp.where(row < classes, head_terms, jnp.where(row == classes, tail, 0.0))
    small[...] = values


def terms_kernel(
    core, parity, rule, masked, recv_a, recv_b, win_two, grad, small, mine, away, win_one, wide, tiles
):
    filter_terms(win_two, grad[...], core, wide, tiles, mine, away)
    pair = jnp.concatenate([split_pair(small[: SMALL // 2]), jnp.zeros((64 - SMALL, LANES), F32)], axis=0).astype(BF16)
    mine[27], away[27] = pair, pair
    below, above = from_sides(parity, recv_a[...], recv_b[...])
    build_windows(masked[...].astype(F32), below[:64], above[:64], rule, win_one)


def three_kernel(
    core, parity, rule, grad_two, recv_a, recv_b, filt, mask, pre, win_one,
    grad_one, mine, away, send_a, send_b, win, wide, tiles,
):
    below, above = from_sides(parity, recv_a[...], recv_b[...])
    build_windows(grad_two[...].astype(F32), below, above, rule, win)
    _, slope = silu_parts(pre[...])
    out = (backward_sum(win, filt) * slope * mask[...]).astype(BF16)
    grad_one[...] = out
    put_layers(out.astype(F32), parity, send_a, send_b)
    filter_terms(win_one, out, core, wide, tiles, mine, away)


def four_kernel(parity, rule, grad_one, recv_a, recv_b, filt, mask, out, win):
    below, above = from_sides(parity, recv_a[...], recv_b[...])
    build_windows(grad_one[...].astype(F32), below, above, rule, win)
    total = backward_sum(win, filt) * mask[...]
    out[...] = total.astype(BF16)


def own_kernel(core, whole, one, two, wide, sems):
    copies = []
    for layer, out in enumerate((one, two)):
        for part in range(3):
            at = pl.ds(TAPS * part, TAPS)
            wide[layer, at] = whole[layer, at].astype(F32) * (1.0 / VOX)
            copies.append(pltpu.make_async_copy(wide.at[layer, at], out.at[core[0], at], sems.at[3 * layer + part]))
            copies[-1].start()
    for copy in copies:
        copy.wait()


def other_kernel(core, whole, one_in, two_in, one, two, wide, sems):
    own_kernel(core, whole, one, two, wide, sems)


def call(kernel, outs, specs, scratch=(), flops=0, params=PARAMS, out_specs=None, alias=None):
    return pl.pallas_call(
        kernel,
        out_shape=outs,
        in_specs=specs,
        out_specs=jax.tree.map(lambda _: VMEM, outs) if out_specs is None else out_specs,
        input_output_aliases=alias or {},
        scratch_shapes=list(scratch),
        compiler_params=params,
        cost_estimate=pl.CostEstimate(flops=flops, bytes_accessed=4_000_000, transcendentals=0),
    )


BLOCK = sds((VOX, LANES), BF16)
WIDE_BLOCK = sds((VOX, LANES), F32)
LAYER = sds((64, LANES), BF16)
FILTER = sds((27, LANES, LANES), BF16)
SIDE = sds((288, LANES), BF16)
WINDOWS = sds((640, TAPS * LANES), BF16)
TERMS = sds((27, 64, LANES), BF16)
GIVEN = sds((28, 64, LANES), BF16)
TILES_SCRATCH = pltpu.VMEM((2, 27, 64, LANES), BF16)
WIN_SCRATCH = pltpu.VMEM((640, TAPS * LANES), BF16)
SEM = pltpu.SemaphoreType.DMA
WIDE_SCRATCH = pltpu.VMEM((640, 3 * LANES), BF16)
CONV = 2 * 27 * VOX * LANES * LANES


def swap_a(value):
    length = lax.axis_size(SPACE)
    return lax.ppermute(value, SPACE, [(i, i ^ 1) for i in range(length)])


def swap_b(value):
    length = lax.axis_size(SPACE)
    pairs = []
    for i in range(length):
        to = i + 1 if i % 2 else i - 1
        for c in range(2):
            pairs.append((2 * i + c, 2 * to + c if 0 <= to < length else 2 * i + 1 - c))
    return lax.ppermute(value, SPACE + ("core",), pairs)


def far_swap(value):
    return lax.ppermute(value, "far", [(0, 1), (1, 0)])


def core_swap(value):
    return lax.ppermute(value, "core", [(0, 1), (1, 0)])


def split_pair(value):
    high = value.astype(BF16).astype(F32)
    return jnp.concatenate([high, value - high], axis=0)


def join_pair(pair):
    return pair[: SMALL // 2] + pair[SMALL // 2 : SMALL]


def pair_kernel(rows, peers, one, one_other, two, two_other, out):
    small = join_pair(two[27].astype(F32)) + join_pair(two_other[27].astype(F32))
    tail = jnp.concatenate([split_pair(small), jnp.zeros((SMALL, LANES), F32)], axis=0)
    halves = [
        a[:27].reshape(27 * 64, LANES).astype(F32) + b[:27].reshape(27 * 64, LANES).astype(F32)
        for a, b in ((one, one_other), (two, two_other))
    ]
    total = jnp.concatenate(halves, axis=0)
    spare = rows * peers - 27 * LANES
    if spare:
        total = jnp.concatenate([total, jnp.zeros((spare, LANES), F32)], axis=0)
    for p in range(peers):
        out[p] = jnp.concatenate([total[p * rows : (p + 1) * rows], tail], axis=0).astype(BF16)


def half_kernel(rows, peers, parts, out):
    total = parts[0].astype(F32)
    for p in range(1, peers):
        total = total + parts[p].astype(F32)
    tail = split_pair(join_pair(total[rows : rows + SMALL]))
    out[...] = jnp.concatenate([total[:rows], tail, jnp.zeros((SMALL, LANES), F32)], axis=0).astype(BF16)


def copies_kernel(rows, peers, classes, mine, other, later_a, later_b, out, head, loss):
    a, b = mine[...].astype(F32), other[...].astype(F32)
    both = (a[:rows] + b[:rows]).astype(BF16)
    for p in range(peers):
        out[p] = both
    tail = join_pair(a[rows:]) + join_pair(b[rows:])
    head[...] = tail[:classes] * (1.0 / VOX)
    last = tail[classes : classes + 1]
    lane = lax.broadcasted_iota(jnp.int32, (1, LANES), 1)
    losses = jnp.sum(jnp.where(lane < classes, last, 0.0), axis=1, keepdims=True)
    counted = jnp.sum(jnp.where(lane == classes, last, 0.0), axis=1, keepdims=True)
    loss[...] = jnp.broadcast_to(losses / counted, (1, LANES))


def local(classes, features, occupancy, labels, rulebook, filter_one, filter_two, head_weight):
    parity = (lax.axis_index(SPACE) % 2).reshape(1).astype(jnp.int32)
    core = lax.axis_index("core").reshape(1).astype(jnp.int32)
    inputs = features.reshape(VOX, LANES), occupancy.reshape(1, VOX), rulebook.reshape(1, 27)
    a, b = call(
        first_kernel,
        (SIDE, SIDE),
        [SMEM] + [ANY] * 3,
        [pltpu.VMEM((VOX, LANES), BF16), pltpu.VMEM((1, VOX), jnp.int32), pltpu.SMEM((1, 27), jnp.int32), SEM((3,))],
        params=ROOMY,
    )(parity, *inputs)
    a, b = swap_a(a), swap_b(b)
    masked, mask, rule, filter_here = call(
        prep_kernel, (BLOCK, WIDE_BLOCK, sds((27, LANES), F32), FILTER), [VMEM] * 4
    )(*inputs, filter_one)
    act_one, act_below, act_above, pre_one = call(
        one_kernel,
        (BLOCK, LAYER, LAYER, WIDE_BLOCK),
        [SMEM] + [VMEM] * 6,
        [WIN_SCRATCH, pltpu.VMEM((128, 27 * LANES), BF16)],
        CONV,
    )(parity, rule, masked, mask, a, b, filter_here)
    win_two, grad_two, small, e, f = call(
        functools.partial(two_kernel, classes),
        (WINDOWS, BLOCK, sds((SMALL, LANES), F32), LAYER, LAYER),
        [SMEM] + [VMEM] * 8,
        flops=CONV,
    )(parity, rule, act_one, act_below, act_above, filter_two, mask, labels.reshape(1, VOX), head_weight.T)
    e, f = swap_a(e), swap_b(f)
    mine_two, away_two, win_one = call(
        terms_kernel, (GIVEN, GIVEN, WINDOWS), [SMEM] * 2 + [VMEM] * 7, [WIDE_SCRATCH, TILES_SCRATCH], CONV
    )(core, parity, rule, masked, a, b, win_two, grad_two, small)
    other_two = core_swap(away_two)
    grad_one, mine_one, away_one, g, h = call(
        three_kernel,
        (BLOCK, TERMS, TERMS, LAYER, LAYER),
        [SMEM] * 2 + [VMEM] * 8,
        [WIN_SCRATCH, WIDE_SCRATCH, TILES_SCRATCH],
        2 * CONV,
    )(core, parity, rule, grad_two, e, f, filter_two, mask, pre_one, win_one)
    g, h = swap_a(g), swap_b(h)
    peers = lax.axis_size("near") * lax.axis_size("x")
    rows = -(-27 * LANES // (peers * 16)) * 16
    chunks = call(
        functools.partial(pair_kernel, rows, peers), sds((peers, rows + 2 * SMALL, LANES), BF16), [VMEM] * 4
    )(mine_one, core_swap(away_one), mine_two, other_two)
    parts = lax.all_to_all(chunks, ("near", "x"), 0, 0, tiled=True)
    part = call(
        functools.partial(half_kernel, rows, peers), sds((rows + 2 * SMALL, LANES), BF16), [VMEM]
    )(parts)
    copies, head_sum, loss = call(
        functools.partial(copies_kernel, rows, peers, classes),
        (sds((peers, rows, LANES), BF16), sds((classes, LANES), F32), sds((1, LANES), F32)),
        [VMEM, VMEM, ANY, ANY],
    )(part, far_swap(part), g, h)
    whole = lax.all_to_all(copies, ("near", "x"), 0, 0, tiled=True)
    whole = whole.reshape(peers * rows, LANES)[: 27 * LANES].reshape(2, 27, 64, LANES)
    whole_other = core_swap(whole)
    grad_in = call(four_kernel, BLOCK, [SMEM] + [VMEM] * 6, [WIN_SCRATCH], CONV)(
        parity, rule, grad_one, g, h, filter_one, mask
    )
    wide = sds((2, 27, 64, LANES), F32)
    room = [pltpu.VMEM((2, 27, 64, LANES), F32), SEM((6,))]
    parts = call(own_kernel, (wide, wide), [SMEM, VMEM], room, out_specs=(ANY, ANY))(core, whole)
    sum_one, sum_two = call(
        other_kernel, (wide, wide), [SMEM, VMEM, ANY, ANY], room, out_specs=(ANY, ANY), alias={2: 0, 3: 1}
    )(1 - core, whole_other, *parts)
    return (
        sum_one.reshape(27, LANES, LANES),
        sum_two.reshape(27, LANES, LANES),
        head_sum.T,
        loss[0, 0],
        grad_in.reshape(features.shape),
    )


def solution(mesh):
    shape = mesh.devices.shape
    inner = Mesh(mesh.devices.reshape(2, shape[0] // 2, shape[1] // 2, 2), ("far", "near", "x", "core"))
    parts = ("x", "core")
    placed = (
        P(parts, SPACE, None, None),
        P(parts, SPACE, None),
        P(parts, SPACE, None),
        P(parts, SPACE, None),
        P(),
        P(),
        P(),
    )

    def whole(features, occupancy, labels, rulebook, filter_one, filter_two, head_weight):
        step = jax.shard_map(
            functools.partial(local, head_weight.shape[1]),
            mesh=inner,
            in_specs=placed,
            out_specs=(P(), P(), P(), P(), P(parts, SPACE, None, None)),
            check_vma=False,
        )
        return step(features, occupancy, labels, rulebook, filter_one, filter_two, head_weight)

    return whole
```

```python
import functools

import jax
import jax.numpy as jnp
from jax import lax
from jax.experimental import pallas as pl
from jax.experimental.pallas import tpu as pltpu
from jax.sharding import Mesh, PartitionSpec as P

EDGE = 8
VOX = 512
LANES = 128
TAPS = 9
SMALL = 8
SPACE = ("far", "near")
F32 = jnp.float32
BF16 = jnp.bfloat16
PARAMS = pltpu.CompilerParams(vmem_limit_bytes=16 * 1024 * 1024)
ROOMY = pltpu.CompilerParams(vmem_limit_bytes=62 * 1024 * 1024)
VMEM = pl.BlockSpec(memory_space=pltpu.VMEM)
ANY = pl.BlockSpec(memory_space=pl.ANY)
SMEM = pl.BlockSpec(memory_space=pltpu.SMEM)


def sds(shape, dtype):
    return jax.ShapeDtypeStruct(shape, dtype)


def contract(a, b, dim_a, dim_b):
    return lax.dot_general(a, b, (((dim_a,), (dim_b,)), ((), ())), preferred_element_type=F32)


def spread_layer(layer):
    return jnp.broadcast_to(layer.astype(F32).reshape(64, 1, LANES), (64, EDGE, LANES))


def from_sides(parity_ref, recv_a, recv_b):
    even = parity_ref[0] == 0
    got_a, got_b = recv_a.astype(F32), recv_b.astype(F32)
    return jnp.where(even, got_b, got_a), jnp.where(even, got_a, got_b)


def build_windows(block, below, above, rule_ref, out_ref):
    cells = block.reshape(64, EDGE, LANES)
    depth = lax.broadcasted_iota(jnp.int32, (1, EDGE, LANES), 1)

    def flag(i, j, k, wanted):
        offset = 9 * i + 3 * j + k
        return jnp.where(rule_ref[offset : offset + 1, :] == wanted, 1.0, 0.0).reshape(1, 1, LANES)

    for k in range(3):
        if k == 1:
            own, other = cells, None
        elif k == 0:
            own, other = pltpu.roll(cells, 1, 1), spread_layer(below)
        else:
            own, other = pltpu.roll(cells, EDGE - 1, 1), spread_layer(above)
        own = own.reshape(EDGE, EDGE, EDGE, LANES)
        if other is not None:
            other = other.reshape(EDGE, EDGE, EDGE, LANES)

        def region(i, j):
            xs = {0: slice(7, 8), 1: slice(0, 8), 2: slice(0, 1)}[i]
            ys = {0: slice(7, 8), 1: slice(0, 8), 2: slice(0, 1)}[j]
            inner = flag(i, j, 1, 0)
            if k == 1:
                return own[xs, ys] * inner[None]
            edge = depth == (0 if k == 0 else EDGE - 1)
            keep = jnp.where(edge, flag(i, j, k, 0), inner)
            take = jnp.where(edge, flag(i, j, k, 1 if k == 0 else 2), 0.0)
            return own[xs, ys] * keep[None] + other[xs, ys] * take[None]

        columns = [jnp.concatenate([region(i, j) for i in range(3)], axis=0).astype(F32) for j in range(3)]
        for j in range(3):
            if j == 0:
                padded = jnp.concatenate([columns[0], columns[1][:, :7]], axis=1)
            elif j == 1:
                padded = columns[1]
            else:
                padded = jnp.concatenate([columns[1][:, 1:], columns[2]], axis=1)
            lane = (3 * j + k) * LANES
            out_ref[:, lane : lane + LANES] = padded.reshape(640, LANES).astype(BF16)


def put_sides(parity_ref, upward, downward, send_a_ref, send_b_ref):
    even = parity_ref[0] == 0
    send_a_ref[...] = jnp.where(even, upward, downward).astype(BF16)
    send_b_ref[...] = jnp.where(even, downward, upward).astype(BF16)


def layers_of(block):
    cells = block.reshape(64, EDGE, LANES)
    return lambda z: cells[:, z, :]


def put_layers(block, parity_ref, send_a_ref, send_b_ref):
    layer = layers_of(block)
    put_sides(parity_ref, layer(EDGE - 1), layer(0), send_a_ref, send_b_ref)


def layer_windows(side, mine, touching, rule, out_ref, row):
    near, behind, wrap = (part.reshape(EDGE, EDGE, LANES) for part in side)
    mine = mine.reshape(EDGE, EDGE, LANES)
    across = 2 if touching == EDGE - 1 else 0
    width = lax.broadcasted_iota(jnp.int32, (1, EDGE, LANES), 1)

    def flag(i, j, k, wanted):
        offset = 9 * i + 3 * j + k
        return jnp.where(rule[offset : offset + 1, :] == wanted, 1.0, 0.0).reshape(1, 1, LANES)

    for k in range(3):
        sources = [(near if k == 1 else behind, 1, 0)]
        if k == across:
            sources = [(wrap, k, 0), (mine, k, 2 if across == 2 else 1)]
        for j in range(3):
            base = first = last = None
            for layer, region, wanted in sources:
                turned = layer if j == 1 else pltpu.roll(layer, 1 if j == 0 else EDGE - 1, 1)

                def gate(i):
                    inner = flag(i, 1, region, wanted)
                    if j == 1:
                        return inner
                    return jnp.where(width == (0 if j == 0 else EDGE - 1), flag(i, j, region, wanted), inner)

                parts = turned * gate(1), turned[7:8] * gate(0), turned[0:1] * gate(2)
                if base is None:
                    base, first, last = parts
                else:
                    base, first, last = base + parts[0], first + parts[1], last + parts[2]
            for i in range(3):
                cells = base
                if i == 0:
                    cells = jnp.concatenate([first, base[:7]], axis=0)
                elif i == 2:
                    cells = jnp.concatenate([base[1:], last], axis=0)
                lane = (9 * i + 3 * j + k) * LANES
                out_ref[row : row + 64, lane : lane + LANES] = cells.reshape(64, LANES).astype(BF16)


def shifted_sum(wide):
    return sum(wide[64 * i : 64 * i + VOX, LANES * i : LANES * (i + 1)] for i in range(3))


def forward_sum(win_ref, filt_ref):
    parts = [filt_ref[TAPS * i : TAPS * (i + 1)].reshape(TAPS * LANES, LANES) for i in range(3)]
    return shifted_sum(jnp.dot(win_ref[...], jnp.concatenate(parts, axis=1), preferred_element_type=F32))


def backward_sum(win_ref, filt_ref):
    parts = [jnp.concatenate([filt_ref[26 - TAPS * i - t] for t in range(TAPS)], axis=1) for i in range(3)]
    return shifted_sum(contract(win_ref[...], jnp.concatenate(parts, axis=0), 1, 1))


def filter_terms(win_ref, grad, core_ref, wide_ref, tiles_ref, mine_ref, away_ref):
    wide_ref[...] = jnp.zeros_like(wide_ref)
    for i in range(3):
        wide_ref[64 * i : 64 * i + VOX, LANES * i : LANES * (i + 1)] = grad
    for t in range(TAPS):
        if t % 9 == 0:
            terms = contract(win_ref[:, LANES * t : LANES * (t + 9)], wide_ref[...], 0, 0)
        term = terms[LANES * (t % 9) : LANES * (t % 9 + 1)]
        for i in range(3):
            tile = term[:, LANES * i : LANES * (i + 1)].astype(BF16)
            at = 2 * (TAPS * i + t)
            tiles_ref[at // 27, at % 27] = tile[:64]
            tiles_ref[(at + 1) // 27, (at + 1) % 27] = tile[64:]
    core = core_ref[0]
    mine_ref[:27] = tiles_ref[core]
    away_ref[:27] = tiles_ref[1 - core]


def silu_parts(pre):
    sigmoid = 1.0 / (1.0 + jnp.exp(-pre))
    return pre * sigmoid, sigmoid * (1.0 + pre * (1.0 - sigmoid))


def filled_rows(occ):
    rows = lax.broadcasted_iota(jnp.int32, (SMALL, VOX), 0)
    occ_rows = jnp.where(rows == 0, jnp.broadcast_to(occ, (SMALL, VOX)), 0).astype(F32).astype(BF16)
    row = lax.broadcasted_iota(jnp.int32, (SMALL, LANES), 0)
    return contract(occ_rows, jnp.where(row == 0, 1.0, 0.0).astype(BF16), 0, 0)


def first_kernel(parity, feat_hbm, occ_hbm, rule_hbm, send_a, send_b, feat, occ, rule, sems):
    copies = [
        pltpu.make_async_copy(feat_hbm, feat, sems.at[0]),
        pltpu.make_async_copy(occ_hbm, occ, sems.at[1]),
        pltpu.make_async_copy(rule_hbm, rule, sems.at[2]),
    ]
    for copy in copies:
        copy.start()
    for copy in copies:
        copy.wait()
    filled = filled_rows(occ[...])
    block = feat[...].astype(F32) * filled
    offsets = lax.broadcasted_iota(jnp.int32, (32, LANES), 0)
    found = jnp.zeros((32, LANES), jnp.int32)
    for o in range(27):
        found = jnp.where(offsets == o, rule[0, o], found)
    found = found.astype(F32)
    layer, held = layers_of(block), layers_of(filled)
    top = EDGE - 1
    upward = jnp.concatenate([layer(top), layer(top - 1), layer(0), held(top), found], axis=0)
    downward = jnp.concatenate([layer(0), layer(1), layer(top), held(0), found], axis=0)
    put_sides(parity, upward, downward, send_a, send_b)


def prep_kernel(feat, occ, found, filt_in, masked, mask, rule, filt):
    filt[...] = filt_in[...]
    row = lax.broadcasted_iota(jnp.int32, (SMALL, 27), 0)
    rule_rows = jnp.where(row == 0, jnp.broadcast_to(found[...], (SMALL, 27)), 0).astype(F32).astype(BF16)
    one_row = lax.broadcasted_iota(jnp.int32, (SMALL, LANES), 0)
    rule[...] = contract(rule_rows, jnp.where(one_row == 0, 1.0, 0.0).astype(BF16), 0, 0)
    filled = filled_rows(occ[...])
    mask[...] = filled
    masked[...] = (feat[...].astype(F32) * filled).astype(BF16)


def one_kernel(parity, rule, masked, mask, recv_a, recv_b, filt, act, act_below, act_above, pre, win, rim):
    below, above = from_sides(parity, recv_a[...], recv_b[...])
    block = masked[...].astype(F32)
    build_windows(block, below[:64], above[:64], rule, win)
    total = forward_sum(win, filt) * mask[...]
    pre[...] = total
    acted, _ = silu_parts(total)
    act[...] = acted.astype(BF16)
    layer = layers_of(block)
    for side, mine, touching, row in ((below, layer(0), EDGE - 1, 0), (above, layer(EDGE - 1), 0, 64)):
        parts = [side[at : at + 64] for at in (0, 64, 128)]
        layer_windows(parts, mine, touching, side[256:288], rim, row)
    total = None
    wide = TAPS * LANES
    for i in range(3):
        weights = filt[TAPS * i : TAPS * (i + 1)].reshape(wide, LANES)
        term = jnp.dot(rim[:, wide * i : wide * (i + 1)], weights, preferred_element_type=F32)
        total = term if total is None else total + term
    for side, row, out in ((below, 0, act_below), (above, 64, act_above)):
        acted, _ = silu_parts(total[row : row + 64] * side[192:256])
        out[...] = acted.astype(BF16)


def two_kernel(
    classes, parity, rule, act_one, act_below, act_above, filt, mask, labels, head_rows,
    win, grad, small, send_a, send_b,
):
    build_windows(act_one[...].astype(F32), act_below[...].astype(F32), act_above[...].astype(F32), rule, win)
    head = jnp.concatenate([head_rows[...].astype(F32), jnp.zeros((LANES - classes, LANES), F32)], axis=0).astype(BF16)
    rows = lax.broadcasted_iota(jnp.int32, (SMALL, VOX), 0)
    hot_rows = jnp.where(rows == jnp.broadcast_to(labels[...], (SMALL, VOX)), 1.0, 0.0).astype(BF16)
    unit_row = lax.broadcasted_iota(jnp.int32, (SMALL, LANES), 0)
    unit_lane = lax.broadcasted_iota(jnp.int32, (SMALL, LANES), 1)
    hot = contract(hot_rows, jnp.where(unit_row == unit_lane, 1.0, 0.0).astype(BF16), 0, 0)
    filled = mask[...]
    pre = forward_sum(win, filt) * filled
    acted, slope = silu_parts(pre)
    acted = acted.astype(BF16)
    lane = lax.broadcasted_iota(jnp.int32, (VOX, LANES), 1)
    logits = contract(acted, head, 1, 1)
    known = lane < classes
    top = jnp.max(jnp.where(known, logits, -jnp.inf), axis=1, keepdims=True)
    powers = jnp.where(known, jnp.exp(jnp.where(known, logits - top, 0.0)), 0.0)
    total_log = top + jnp.log(jnp.sum(powers, axis=1, keepdims=True))
    chances = jnp.where(known, jnp.exp(jnp.where(known, logits - total_log, 0.0)), 0.0)
    dlogits = (chances - hot) * filled
    high = dlogits.astype(BF16)
    low = (dlogits - high.astype(F32)).astype(BF16)
    back = jnp.dot(high, head, preferred_element_type=F32) + jnp.dot(low, head, preferred_element_type=F32)
    out = (back * slope * filled).astype(BF16)
    grad[...] = out
    put_layers(out.astype(F32), parity, send_a, send_b)
    head_terms = (contract(high, acted, 0, 0) + contract(low, acted, 0, 0))[:SMALL]
    losses = jnp.sum((total_log - logits) * hot * filled, axis=0, keepdims=True)
    counted = jnp.sum(filled, axis=0, keepdims=True)
    tail = jnp.where(lane[:1] < classes, losses, jnp.where(lane[:1] == classes, counted, 0.0))
    row = lax.broadcasted_iota(jnp.int32, (SMALL, LANES), 0)
    values = jnp.where(row < classes, head_terms, jnp.where(row == classes, tail, 0.0))
    small[...] = values


def terms_kernel(
    core, parity, rule, masked, recv_a, recv_b, win_two, grad, small, mine, away, win_one, wide, tiles
):
    filter_terms(win_two, grad[...], core, wide, tiles, mine, away)
    pair = jnp.concatenate([split_pair(small[: SMALL // 2]), jnp.zeros((64 - SMALL, LANES), F32)], axis=0).astype(BF16)
    mine[27], away[27] = pair, pair
    below, above = from_sides(parity, recv_a[...], recv_b[...])
    build_windows(masked[...].astype(F32), below[:64], above[:64], rule, win_one)


def three_kernel(
    core, parity, rule, grad_two, recv_a, recv_b, filt, mask, pre, win_one,
    grad_one, mine, away, send_a, send_b, win, wide, tiles,
):
    below, above = from_sides(parity, recv_a[...], recv_b[...])
    build_windows(grad_two[...].astype(F32), below, above, rule, win)
    _, slope = silu_parts(pre[...])
    out = (backward_sum(win, filt) * slope * mask[...]).astype(BF16)
    grad_one[...] = out
    put_layers(out.astype(F32), parity, send_a, send_b)
    filter_terms(win_one, out, core, wide, tiles, mine, away)


def four_kernel(parity, rule, grad_one, recv_a, recv_b, filt, mask, out, win):
    below, above = from_sides(parity, recv_a[...], recv_b[...])
    build_windows(grad_one[...].astype(F32), below, above, rule, win)
    total = backward_sum(win, filt) * mask[...]
    out[...] = total.astype(BF16)


def own_kernel(core, whole, one, two, wide, sems):
    copies = []
    for layer, out in enumerate((one, two)):
        for part in range(3):
            at = pl.ds(TAPS * part, TAPS)
            wide[layer, at] = whole[layer, at].astype(F32) * (1.0 / VOX)
            copies.append(pltpu.make_async_copy(wide.at[layer, at], out.at[core[0], at], sems.at[3 * layer + part]))
            copies[-1].start()
    for copy in copies:
        copy.wait()


def other_kernel(core, whole, one_in, two_in, one, two, wide, sems):
    own_kernel(core, whole, one, two, wide, sems)


def call(kernel, outs, specs, scratch=(), flops=0, params=PARAMS, out_specs=None, alias=None):
    return pl.pallas_call(
        kernel,
        out_shape=outs,
        in_specs=specs,
        out_specs=jax.tree.map(lambda _: VMEM, outs) if out_specs is None else out_specs,
        input_output_aliases=alias or {},
        scratch_shapes=list(scratch),
        compiler_params=params,
        cost_estimate=pl.CostEstimate(flops=flops, bytes_accessed=4_000_000, transcendentals=0),
    )


BLOCK = sds((VOX, LANES), BF16)
WIDE_BLOCK = sds((VOX, LANES), F32)
LAYER = sds((64, LANES), BF16)
FILTER = sds((27, LANES, LANES), BF16)
SIDE = sds((288, LANES), BF16)
WINDOWS = sds((640, TAPS * LANES), BF16)
TERMS = sds((27, 64, LANES), BF16)
GIVEN = sds((28, 64, LANES), BF16)
TILES_SCRATCH = pltpu.VMEM((2, 27, 64, LANES), BF16)
WIN_SCRATCH = pltpu.VMEM((640, TAPS * LANES), BF16)
SEM = pltpu.SemaphoreType.DMA
WIDE_SCRATCH = pltpu.VMEM((640, 3 * LANES), BF16)
CONV = 2 * 27 * VOX * LANES * LANES


def swap_a(value):
    length = lax.axis_size(SPACE)
    return lax.ppermute(value, SPACE, [(i, i ^ 1) for i in range(length)])


def swap_b(value):
    length = lax.axis_size(SPACE)
    pairs = []
    for i in range(length):
        to = i + 1 if i % 2 else i - 1
        for c in range(2):
            pairs.append((2 * i + c, 2 * to + c if 0 <= to < length else 2 * i + 1 - c))
    return lax.ppermute(value, SPACE + ("core",), pairs)


def far_swap(value):
    return lax.ppermute(value, "far", [(0, 1), (1, 0)])


def core_swap(value):
    return lax.ppermute(value, "core", [(0, 1), (1, 0)])


def split_pair(value):
    high = value.astype(BF16).astype(F32)
    return jnp.concatenate([high, value - high], axis=0)


def join_pair(pair):
    return pair[: SMALL // 2] + pair[SMALL // 2 : SMALL]


def pair_kernel(rows, peers, one, one_other, two, two_other, out):
    small = join_pair(two[27].astype(F32)) + join_pair(two_other[27].astype(F32))
    tail = jnp.concatenate([split_pair(small), jnp.zeros((SMALL, LANES), F32)], axis=0)
    halves = [
        a[:27].reshape(27 * 64, LANES).astype(F32) + b[:27].reshape(27 * 64, LANES).astype(F32)
        for a, b in ((one, one_other), (two, two_other))
    ]
    total = jnp.concatenate(halves, axis=0)
    spare = rows * peers - 27 * LANES
    if spare:
        total = jnp.concatenate([total, jnp.zeros((spare, LANES), F32)], axis=0)
    for p in range(peers):
        out[p] = jnp.concatenate([total[p * rows : (p + 1) * rows], tail], axis=0).astype(BF16)


def half_kernel(rows, peers, parts, out):
    total = parts[0].astype(F32)
    for p in range(1, peers):
        total = total + parts[p].astype(F32)
    tail = split_pair(join_pair(total[rows : rows + SMALL]))
    out[...] = jnp.concatenate([total[:rows], tail, jnp.zeros((SMALL, LANES), F32)], axis=0).astype(BF16)


def copies_kernel(rows, peers, classes, mine, other, later_a, later_b, out, head, loss):
    a, b = mine[...].astype(F32), other[...].astype(F32)
    both = (a[:rows] + b[:rows]).astype(BF16)
    for p in range(peers):
        out[p] = both
    tail = join_pair(a[rows:]) + join_pair(b[rows:])
    head[...] = tail[:classes] * (1.0 / VOX)
    last = tail[classes : classes + 1]
    lane = lax.broadcasted_iota(jnp.int32, (1, LANES), 1)
    losses = jnp.sum(jnp.where(lane < classes, last, 0.0), axis=1, keepdims=True)
    counted = jnp.sum(jnp.where(lane == classes, last, 0.0), axis=1, keepdims=True)
    loss[...] = jnp.broadcast_to(losses / counted, (1, LANES))


def local(classes, features, occupancy, labels, rulebook, filter_one, filter_two, head_weight):
    parity = (lax.axis_index(SPACE) % 2).reshape(1).astype(jnp.int32)
    core = lax.axis_index("core").reshape(1).astype(jnp.int32)
    inputs = features.reshape(VOX, LANES), occupancy.reshape(1, VOX), rulebook.reshape(1, 27)
    a, b = call(
        first_kernel,
        (SIDE, SIDE),
        [SMEM] + [ANY] * 3,
        [pltpu.VMEM((VOX, LANES), BF16), pltpu.VMEM((1, VOX), jnp.int32), pltpu.SMEM((1, 27), jnp.int32), SEM((3,))],
        params=ROOMY,
    )(parity, *inputs)
    a, b = swap_a(a), swap_b(b)
    masked, mask, rule, filter_here = call(
        prep_kernel, (BLOCK, WIDE_BLOCK, sds((27, LANES), F32), FILTER), [VMEM] * 4
    )(*inputs, filter_one)
    act_one, act_below, act_above, pre_one = call(
        one_kernel,
        (BLOCK, LAYER, LAYER, WIDE_BLOCK),
        [SMEM] + [VMEM] * 6,
        [WIN_SCRATCH, pltpu.VMEM((128, 27 * LANES), BF16)],
        CONV,
    )(parity, rule, masked, mask, a, b, filter_here)
    win_two, grad_two, small, e, f = call(
        functools.partial(two_kernel, classes),
        (WINDOWS, BLOCK, sds((SMALL, LANES), F32), LAYER, LAYER),
        [SMEM] + [VMEM] * 8,
        flops=CONV,
    )(parity, rule, act_one, act_below, act_above, filter_two, mask, labels.reshape(1, VOX), head_weight.T)
    e, f = swap_a(e), swap_b(f)
    mine_two, away_two, win_one = call(
        terms_kernel, (GIVEN, GIVEN, WINDOWS), [SMEM] * 2 + [VMEM] * 7, [WIDE_SCRATCH, TILES_SCRATCH], CONV
    )(core, parity, rule, masked, a, b, win_two, grad_two, small)
    other_two = core_swap(away_two)
    grad_one, mine_one, away_one, g, h = call(
        three_kernel,
        (BLOCK, TERMS, TERMS, LAYER, LAYER),
        [SMEM] * 2 + [VMEM] * 8,
        [WIN_SCRATCH, WIDE_SCRATCH, TILES_SCRATCH],
        2 * CONV,
    )(core, parity, rule, grad_two, e, f, filter_two, mask, pre_one, win_one)
    g, h = swap_a(g), swap_b(h)
    peers = lax.axis_size("near") * lax.axis_size("x")
    rows = -(-27 * LANES // (peers * 16)) * 16
    chunks = call(
        functools.partial(pair_kernel, rows, peers), sds((peers, rows + 2 * SMALL, LANES), BF16), [VMEM] * 4
    )(mine_one, core_swap(away_one), mine_two, other_two)
    parts = lax.all_to_all(chunks, ("near", "x"), 0, 0, tiled=True)
    part = call(
        functools.partial(half_kernel, rows, peers), sds((rows + 2 * SMALL, LANES), BF16), [VMEM]
    )(parts)
    copies, head_sum, loss = call(
        functools.partial(copies_kernel, rows, peers, classes),
        (sds((peers, rows, LANES), BF16), sds((classes, LANES), F32), sds((1, LANES), F32)),
        [VMEM, VMEM, ANY, ANY],
    )(part, far_swap(part), g, h)
    whole = lax.all_to_all(copies, ("near", "x"), 0, 0, tiled=True)
    whole = whole.reshape(peers * rows, LANES)[: 27 * LANES].reshape(2, 27, 64, LANES)
    whole_other = core_swap(whole)
    grad_in = call(four_kernel, BLOCK, [SMEM] + [VMEM] * 6, [WIN_SCRATCH], CONV)(
        parity, rule, grad_one, g, h, filter_one, mask
    )
    wide = sds((2, 27, 64, LANES), F32)
    room = [pltpu.VMEM((2, 27, 64, LANES), F32), SEM((6,))]
    parts = call(own_kernel, (wide, wide), [SMEM, VMEM], room, out_specs=(ANY, ANY))(core, whole)
    sum_one, sum_two = call(
        other_kernel, (wide, wide), [SMEM, VMEM, ANY, ANY], room, out_specs=(ANY, ANY), alias={2: 0, 3: 1}
    )(1 - core, whole_other, *parts)
    return (
        sum_one.reshape(27, LANES, LANES),
        sum_two.reshape(27, LANES, LANES),
        head_sum.T,
        loss[0, 0],
        grad_in.reshape(features.shape),
    )


def solution(mesh):
    shape = mesh.devices.shape
    inner = Mesh(mesh.devices.reshape(2, shape[0] // 2, shape[1] // 2, 2), ("far", "near", "x", "core"))
    parts = ("x", "core")
    placed = (
        P(parts, SPACE, None, None),
        P(parts, SPACE, None),
        P(parts, SPACE, None),
        P(parts, SPACE, None),
        P(),
        P(),
        P(),
    )

    def whole(features, occupancy, labels, rulebook, filter_one, filter_two, head_weight):
        step = jax.shard_map(
            functools.partial(local, head_weight.shape[1]),
            mesh=inner,
            in_specs=placed,
            out_specs=(P(), P(), P(), P(), P(parts, SPACE, None, None)),
            check_vma=False,
        )
        return step(features, occupancy, labels, rulebook, filter_one, filter_two, head_weight)

    return whole
```
